128 devices in a mesh: seq: 16 (over y_lo, z, core), mp: 8 (over y_hi, x).
Axes of the slice: x: 4, y: 4 (y_hi: 2, y_lo: 2; y = y_hi * 2 + y_lo), z: 4, core: 2. Of those that a mesh axis runs over, the one named last changes fastest.
Arguments:
- nucleotide_codes: int32 [1048576], P('seq'), may hold values from 0 to 3, as said below
- segment_encoder_map: bfloat16 [512, 1536], P(None, 'mp'), may hold values from -0.5 to 0.5
- mixing_norm_scale: bfloat16 [1536], replicated, may hold values from 0.099609375 to 1.8984375
- asker_probe_content_map: bfloat16 [1536, 3584], P(None, 'mp'), may hold values from -0.15309311 to 0.15309311
- logit_sharpness: float32 [8], P('mp'), may hold values from 3 to 30
- mixing_exit_map: bfloat16 [1536, 1536], P('mp'), may hold values from -0.15625 to 0.15625
- perceptron_norm_scale: bfloat16 [1536], replicated, may hold values from 0.099609375 to 1.8984375
- perceptron_widening_map: bfloat16 [1536, 3072], P(None, 'mp'), may hold values from -0.15625 to 0.15625
- perceptron_narrowing_map: bfloat16 [3072, 1536], P('mp'), may hold values from -0.109375 to 0.109375
- widening_kernel: bfloat16 [5, 1536, 768], P(None, None, 'mp'), may hold values from -0.0625 to 0.0625
Outputs:
- decoded: bfloat16 [768, 16384], P('mp', 'seq')
The draws below stay inside these ranges and needn't reach their ends.
Inputs may be any that keep to these rules, and one draw needn't show every extreme that they name: `nucleotide_codes`: codes of the bases A, C, G, T; the mix of bases differs from region to region of the sequence.
All inputs are finite; a program needn't handle non-finite values.
Results may differ from the reference program's by a relative error of at most 0.011.
Values may be sent and summed in bfloat16 or wider, within the bound.
A program may use at most 64 MiB of HBM per device.

```python
import math
import jax
import jax.numpy as jnp
from jax import lax

D = 1536
NUM_LENSES = 8
PROBE_DIM = 128
VALUE = 192
FF = 3072
C_OUT = 768
PATCH = 128
WIDTH = 5
TOK_DEV = 512
TOKENS = 8192
BASES = 1048576
POSITIONS = 16384


def draw_nucleotide_codes(key, part):
    key = jax.random.fold_in(key, 7)
    region = PATCH * TOK_DEV // 4
    regions = BASES // region
    key_list = jax.random.split(key, 7)
    weights = jax.random.randint(key_list[0], (regions, 4), 1, 17)
    ladder = jnp.cumsum(weights, axis=1)
    pick_values = jax.random.randint(key_list[1], (regions, region), 0, ladder[:, 3:4])
    base_codes = jnp.sum((pick_values[:, :, None] >= ladder[:, None, :3]).astype(jnp.int32), axis=2)
    base_codes = base_codes.reshape(TOKENS, PATCH)
    source_pool = jax.random.randint(key_list[2], (TOKENS // 16,), 0, TOKENS)
    choose = jax.random.randint(key_list[3], (TOKENS,), 0, TOKENS // 16)
    source = source_pool[choose]
    planted = jax.random.randint(key_list[4], (TOKENS,), 0, 4) == 0
    copied = base_codes[source]
    fresh_codes = jax.random.randint(key_list[5], (TOKENS, PATCH), 0, 4)
    mutate = jax.random.randint(key_list[6], (TOKENS, PATCH), 0, 8) == 0
    copied = jnp.where(mutate, fresh_codes, copied)
    all_codes = jnp.where(planted[:, None], copied, base_codes)
    return all_codes.reshape(BASES).astype(jnp.int32)


def draw_asker_probe_content_map(key, part):
    key = jax.random.fold_in(key, 11)
    first_key, second_key, third_key = jax.random.split(key, 3)
    probe_part = jax.random.truncated_normal(first_key, -4.0, 4.0, (D, NUM_LENSES, PROBE_DIM), jnp.float32)
    blur_noise = jax.random.truncated_normal(second_key, -4.0, 4.0, (D, NUM_LENSES, PROBE_DIM), jnp.float32)
    content_part = jax.random.truncated_normal(third_key, -4.0, 4.0, (D, NUM_LENSES, VALUE), jnp.float32)
    tie_weight = 0.3
    asker_part = probe_part + tie_weight * blur_noise
    combined = jnp.concatenate([asker_part, probe_part, content_part], axis=2) * D ** (-0.5)
    return combined.reshape(D, NUM_LENSES * (2 * PROBE_DIM + VALUE)).astype(jnp.bfloat16)


def block_scale(stream_key, dims, pieces, low, largest):
    loudness, own = 1.0, jax.random.fold_in(stream_key, 6)
    for dim, shards_of in pieces:
        steps = jnp.exp(jax.random.uniform(jax.random.fold_in(own, dim), (shards_of,), jnp.float32, low / len(pieces), largest / len(pieces)))
        loudness = loudness * jnp.repeat(steps, dims[dim] // shards_of).reshape([-1 if axis == dim else 1 for axis in range(len(dims))])
    return loudness


def noise(stream_key, extent, width, limit, shards=(), kind=jnp.bfloat16):
    drawn = jax.random.normal(stream_key, extent, jnp.float32) * width
    if len(shards) > 0:
        drawn = block_scale(stream_key, extent, shards, -0.22, 0.18) * drawn
    return jnp.clip(drawn, min=-limit, max=limit).astype(kind)


def setup_inputs(seed: int = 0) -> dict:
    keys = jax.random.split(jax.random.key(seed), 11)
    return {
        "nucleotide_codes": draw_nucleotide_codes(jax.random.fold_in(keys[10], 71), 0),
        "segment_encoder_map": noise(keys[1], (4 * PATCH, D), PATCH ** -0.5, 0.5, ((1, 8),)),
        "mixing_norm_scale": jnp.clip(1.0 + 0.18 * jax.random.normal(keys[2], (D,), jnp.float32), 0.099609375, 1.8984375).astype(jnp.bfloat16),
        "asker_probe_content_map": draw_asker_probe_content_map(jax.random.fold_in(keys[10], 71), 0),
        "logit_sharpness": jnp.clip(jnp.exp(math.log(30.0) - 2.3025851 * jax.random.uniform(keys[4], (NUM_LENSES,), jnp.float32) ** block_scale(keys[4], (NUM_LENSES,), ((0, 8),), -0.2, 0.2)), 3.0, 30.0),
        "mixing_exit_map": noise(keys[5], (NUM_LENSES * VALUE, D), (NUM_LENSES * VALUE) ** -0.5, 0.15625, ((0, 8),)),
        "perceptron_norm_scale": jnp.clip(1.0 + 0.18 * jax.random.normal(keys[6], (D,), jnp.float32), 0.099609375, 1.8984375).astype(jnp.bfloat16),
        "perceptron_widening_map": noise(keys[7], (D, FF), D ** -0.5, 0.15625, ((1, 8),)),
        "perceptron_narrowing_map": noise(keys[8], (FF, D), FF ** -0.5, 0.109375, ((0, 8),)),
        "widening_kernel": noise(keys[9], (WIDTH, D, C_OUT), (WIDTH * D) ** -0.5, 0.0625, ((2, 8),)),
    }


epsilon = 1e-06

def rms_inverse(content_vectors):
    return lax.rsqrt(lax.optimization_barrier(jnp.mean(content_vectors * content_vectors, axis=-1)) + epsilon)

def reference(nucleotide_codes, segment_encoder_map, mixing_norm_scale, asker_probe_content_map, logit_sharpness, mixing_exit_map, perceptron_norm_scale, perceptron_widening_map, perceptron_narrowing_map, widening_kernel):
    codes = nucleotide_codes.reshape(TOKENS, PATCH)
    onehot = (codes[:, :, None] == jnp.arange(4, dtype=jnp.int32)).astype(jnp.bfloat16).reshape(TOKENS, PATCH * 4)
    stream = jnp.dot(onehot, segment_encoder_map, preferred_element_type=jnp.float32).astype(jnp.bfloat16)
    wide = stream.astype(jnp.float32)
    first_scale = rms_inverse(wide)
    scaled = (wide * mixing_norm_scale.astype(jnp.float32)).astype(jnp.bfloat16)
    affine_transform = jnp.dot(scaled, asker_probe_content_map, preferred_element_type=jnp.float32) * first_scale[:, None]
    affine_transform = affine_transform.reshape(TOKENS, NUM_LENSES, 2 * PROBE_DIM + VALUE)
    asker_vectors = affine_transform[:, :, :PROBE_DIM]
    probe_vectors = affine_transform[:, :, PROBE_DIM:2 * PROBE_DIM]
    content_vectors = affine_transform[:, :, 2 * PROBE_DIM:].astype(jnp.bfloat16)
    asker_vectors = (asker_vectors * rms_inverse(asker_vectors)[..., None]).astype(jnp.bfloat16)
    probe_vectors = (probe_vectors * rms_inverse(probe_vectors)[..., None]).astype(jnp.bfloat16)
    block = math.gcd(TOKENS, 512)

    def lone_lens(operands):
        head_query, head_keys, head_values, resolution_ratio = operands
        flipped = head_keys.T

        def one_block(rows):
            scores = jnp.dot(rows, flipped, preferred_element_type=jnp.float32) * (resolution_ratio / PROBE_DIM)
            weights = jnp.exp(scores)
            totals = lax.optimization_barrier(jnp.sum(weights, axis=1))
            numer = jnp.dot(weights.astype(jnp.bfloat16), head_values, preferred_element_type=jnp.float32)
            return (numer / totals[:, None]).astype(jnp.bfloat16)
        return lax.map(one_block, head_query.reshape(TOKENS // block, block, PROBE_DIM)).reshape(TOKENS, VALUE)
    mixing_result = lax.map(lone_lens, (asker_vectors.transpose(1, 0, 2), probe_vectors.transpose(1, 0, 2), content_vectors.transpose(1, 0, 2), logit_sharpness))
    mixing_result = mixing_result.transpose(1, 0, 2).reshape(TOKENS, NUM_LENSES * VALUE)
    mixed = (wide + jnp.dot(mixing_result, mixing_exit_map, preferred_element_type=jnp.float32)).astype(jnp.bfloat16)
    mixed_wide = mixed.astype(jnp.float32)
    second_scale = rms_inverse(mixed_wide)
    scaled_two = (mixed_wide * perceptron_norm_scale.astype(jnp.float32)).astype(jnp.bfloat16)
    inner = jnp.maximum(jnp.dot(scaled_two, perceptron_widening_map, preferred_element_type=jnp.float32) * second_scale[:, None], 0.0).astype(jnp.bfloat16)
    final = (mixed_wide + jnp.dot(inner, perceptron_narrowing_map, preferred_element_type=jnp.float32)).astype(jnp.bfloat16)
    doubled = jnp.repeat(final, 2, axis=0)
    padded = jnp.pad(doubled, ((2, 2), (0, 0)))
    total = jnp.zeros((POSITIONS, C_OUT), jnp.float32)
    for shift in range(WIDTH):
        total = total + jnp.dot(padded[shift:shift + POSITIONS], widening_kernel[shift], preferred_element_type=jnp.float32)
    return total.T.astype(jnp.bfloat16)
```

```python
import functools

import jax
import jax.numpy as jnp
from jax import lax
from jax.experimental import pallas as pl
from jax.experimental.pallas import tpu as pltpu
from jax.sharding import PartitionSpec as P

MESH = pl.DeviceIdType.MESH
BF = jnp.bfloat16
F32 = jnp.float32

D = 1536
T = 512
PROBE = 128
VALUE = 192
HIDDEN = 384
OUTS = 96
PATCH = 128
EPS = 1e-06
LOG2E = 1.4426950408889634


def dot(a, b):
    return jnp.dot(a, b, preferred_element_type=F32)


def dot_nt(a, b):
    return lax.dot_general(a, b, (((1,), (1,)), ((), ())), preferred_element_type=F32)


def dot_tn(a, b):
    return lax.dot_general(a, b, (((0,), (0,)), ((), ())), preferred_element_type=F32)


def one_hot_codes(codes):
    wide = codes.astype(F32)
    parts = [jnp.where(wide == float(b), 1.0, 0.0).astype(BF) for b in range(4)]
    return jnp.concatenate(parts, axis=1)


def gain_columns(row, width):
    spread = jnp.broadcast_to(row, (16, D)).astype(BF)
    return dot_tn(spread, jnp.full((16, width), 1.0 / 16.0, BF))


def token_columns(row, width):
    high = row.astype(BF)
    low = (row - high.astype(F32)).astype(BF)
    both = jnp.concatenate(
        [jnp.broadcast_to(high, (16, T)), jnp.broadcast_to(low, (16, T))], axis=0
    )
    return dot_tn(both, jnp.full((32, width), 1.0 / 16.0, BF))


def kernel(
    codes_hbm,
    e_hbm,
    g1_ref,
    w_hbm,
    sharp_ref,
    exit_hbm,
    g2_ref,
    widen_hbm,
    narrow_hbm,
    conv_hbm,
    out_ref,
    codes_i,
    codes_all,
    codes_sib,
    e_loc,
    et_full,
    w_loc,
    wg_t,
    m_t,
    exit_full,
    exit_t,
    stream_t,
    u_all,
    u_sib,
    keys,
    vals,
    queries,
    acc,
    part_recv,
    att_full,
    mixed_t,
    widen_loc,
    widen_t,
    narrow_loc,
    narrow_t,
    inner_t,
    rs_send,
    rs_recv,
    fin_full,
    conv_loc,
    conv_t,
    taps,
    edge_send,
    edge_recv,
    in_sem,
    codes_ss,
    codes_rs,
    e_ss,
    e_rs,
    ef_ss,
    ef_rs,
    x_ss,
    x_rs,
    xf_ss,
    xf_rs,
    u_ss,
    u_rs,
    p_ss,
    p_rs,
    att_ss,
    att_rs,
    sum_ss,
    sum_rs,
    fin_ss,
    fin_rs,
    edge_ss,
    edge_rs,
):
    s = lax.axis_index("seq")
    m = lax.axis_index("mp")
    core = s % 2
    j = s // 2
    sib = s + 1 - 2 * core
    far = (s + 15 + 2 * core) % 16
    hi = m // 4

    def weight_peer(d):
        m2 = (m + d) % 8
        return ((s + 8 * ((m2 // 4 + hi) % 2)) % 16, m2)

    def seq_peer(d):
        return (2 * ((j + d) % 8) + core, m)

    def mp_peer(d):
        return (s, (m + d) % 8)

    def send(src, dst, ss, rs, dev):
        copy = pltpu.make_async_remote_copy(
            src_ref=src, dst_ref=dst, send_sem=ss, recv_sem=rs, device_id=dev, device_id_type=MESH
        )
        return copy

    pending = []

    def push(src, dst, ss, rs, dev):
        copy = send(src, dst, ss, rs, dev)
        copy.start()
        pending.append(copy)

    def arrive(dst, ss, rs):
        send(dst, dst, ss, rs, (sib, m)).wait_recv()

    local = [
        pltpu.make_async_copy(codes_hbm, codes_i, in_sem.at[0]),
        pltpu.make_async_copy(e_hbm, e_loc, in_sem.at[1]),
        pltpu.make_async_copy(w_hbm, w_loc, in_sem.at[2]),
        pltpu.make_async_copy(
            exit_hbm, exit_full.at[pl.ds(pl.multiple_of(m * 192, 192), 192)], in_sem.at[3]
        ),
        pltpu.make_async_copy(widen_hbm, widen_loc, in_sem.at[4]),
        pltpu.make_async_copy(narrow_hbm, narrow_loc, in_sem.at[5]),
        pltpu.make_async_copy(conv_hbm, conv_loc, in_sem.at[6]),
    ]
    for copy in local:
        copy.start()

    barrier = pltpu.get_barrier_semaphore()
    greet = [(s, (m + d) % 8) for d in range(1, 8)]
    greet += [((s + 8) % 16, (1 - hi) * 4 + x) for x in range(4)]
    greet += [seq_peer(d) for d in range(1, 8)]
    greet += [(sib, m), (far, m)]
    for dev in greet:
        pl.semaphore_signal(barrier, inc=1, device_id=dev, device_id_type=MESH)

    local[0].wait()
    codes_all[j] = codes_i[...].astype(BF)
    local[1].wait()
    rows = lax.broadcasted_iota(jnp.int32, (T, T), 0)
    cols = lax.broadcasted_iota(jnp.int32, (T, T), 1)
    order = jnp.where(rows == 4 * (cols % PATCH) + cols // PATCH, 1.0, 0.0).astype(BF)
    et_full[pl.ds(pl.multiple_of(m * 192, 192), 192), :] = dot_tn(e_loc[...], order).astype(BF)

    pl.semaphore_wait(barrier, len(greet))

    def half(ref, shard, c):
        return ref.at[pl.ds(pl.multiple_of(shard * 192 + c * 96, 96), 96)]

    for d in range(1, 8):
        mine = half(et_full, m, core)
        push(mine, mine, e_ss.at[d], e_rs.at[d], weight_peer(d))
    push(codes_all.at[j], codes_sib, codes_ss.at[0], codes_rs.at[0], (sib, m))
    for d in range(1, 8):
        push(codes_all.at[j], codes_all.at[j], codes_ss.at[d], codes_rs.at[d], seq_peer(d))
    local[3].wait()
    for d in range(1, 8):
        mine = half(exit_full, m, core)
        push(mine, mine, x_ss.at[d], x_rs.at[d], weight_peer(d))

    local[2].wait()
    gain = gain_columns(g1_ref[...], 128)
    scaled_w = (
        w_loc[...].astype(F32) * jnp.concatenate([gain] * 3 + [gain[:, :64]], axis=1)
    ).astype(BF)
    wg_t[0:448, :] = scaled_w.T
    wg_t[448:512, :] = jnp.zeros((64, D), BF)

    for d in range(1, 8):
        shard = (m + 8 - d) % 8
        landed = half(et_full, shard, core)
        arrive(landed, e_ss.at[d], e_rs.at[d])
        push(landed, landed, ef_ss.at[d], ef_rs.at[d], (sib, m))
    for d in range(1, 8):
        landed = half(et_full, (m + 8 - d) % 8, 1 - core)
        arrive(landed, ef_ss.at[d], ef_rs.at[d])

    mine_hot = one_hot_codes(codes_all[j])

    def stream_step(i, total):
        at = pl.ds(pl.multiple_of(i * 256, 256), 256)
        tile = dot_nt(et_full[at, :], mine_hot).astype(BF)
        stream_t[at, :] = tile
        wide = tile.astype(F32)
        return total + jnp.sum(wide * wide, axis=0, keepdims=True)

    squares = lax.fori_loop(0, D // 256, stream_step, jnp.zeros((1, T), F32))
    u_all[j] = jnp.broadcast_to(squares / D + EPS, (8, T))
    push(u_all.at[j], u_sib, u_ss.at[0], u_rs.at[0], (sib, m))
    for d in range(1, 8):
        push(u_all.at[j], u_all.at[j], u_ss.at[d], u_rs.at[d], seq_peer(d))

    m_t[...] = dot(wg_t[...], et_full[...]).astype(BF)

    lanes = lax.broadcasted_iota(jnp.int32, (T, 256), 1)

    def keys_values(block, at):
        hot = one_hot_codes(codes_all[block])
        raw = dot_nt(hot, m_t[128:512, :])
        spread = token_columns(u_all[block][0:1], 128)
        key = raw[:, :128]
        mean = jnp.mean(key * key, axis=1, keepdims=True)
        keys[at, :] = (key * lax.rsqrt(mean + EPS * spread)).astype(BF)
        inverse = lax.rsqrt(spread)
        value = raw[:, 128:] * jnp.concatenate([inverse, inverse], axis=1)
        vals[at, :] = jnp.where(lanes < VALUE, value, 1.0).astype(BF)

    factor = sharp_ref[0] * (LOG2E / PROBE)

    def make_queries(slot, codes, u_row):
        raw = dot_nt(one_hot_codes(codes), m_t[0:128, :])
        spread = token_columns(u_row, 128)
        mean = jnp.mean(raw * raw, axis=1, keepdims=True)
        queries[slot] = (raw * (lax.rsqrt(mean + EPS * spread) * factor)).astype(BF)

    keys_values(j, pl.ds(0, T))
    make_queries(1, codes_all[j], u_all[j][0:1])
    arrive(codes_sib, codes_ss.at[0], codes_rs.at[0])
    arrive(u_sib, u_ss.at[0], u_rs.at[0])
    make_queries(0, codes_sib[...], u_sib[0:1])
    for d in range(1, 8):
        block = (j + 8 - d) % 8
        arrive(codes_all.at[block], codes_ss.at[d], codes_rs.at[d])
        arrive(u_all.at[block], u_ss.at[d], u_rs.at[d])
        keys_values(block, pl.ds(d * T, T))

    def attend(slot):
        def chunk(q, _):
            at = pl.ds(pl.multiple_of(q * 256, 256), 256)
            asked = queries[slot, at, :]

            def step(k, total):
                span = pl.ds(pl.multiple_of(k * 1024, 1024), 1024)
                weights = jnp.exp2(dot_nt(asked, keys[span, :])).astype(BF)
                return total + dot(weights, vals[span, :])

            acc[slot, at, :] = lax.fori_loop(0, 4, step, jnp.zeros((256, 256), F32), unroll=True)
            return 0

        lax.fori_loop(0, 2, chunk, 0)

    attend(0)
    push(acc.at[0], part_recv, p_ss.at[0], p_rs.at[0], (sib, m))

    for d in range(1, 8):
        landed = half(exit_full, (m + 8 - d) % 8, core)
        arrive(landed, x_ss.at[d], x_rs.at[d])
        push(landed, landed, xf_ss.at[d], xf_rs.at[d], (sib, m))

    attend(1)
    arrive(part_recv, p_ss.at[0], p_rs.at[0])
    whole = acc[1] + part_recv[...]
    attended = whole[:, :VALUE] / whole[:, VALUE : VALUE + 1]
    my_rows = pl.ds(pl.multiple_of(m * 192, 192), 192)
    att_full[my_rows, :] = attended.astype(BF).T
    for d in range(1, 8):
        push(
            att_full.at[my_rows], att_full.at[my_rows], att_ss.at[d], att_rs.at[d], mp_peer(d)
        )

    local[4].wait()
    gain = gain_columns(g2_ref[...], 128)
    widen_t[...] = (
        (widen_loc[...].astype(F32) * jnp.concatenate([gain] * 3, axis=1)).astype(BF).T
    )
    local[5].wait()
    narrow_t[...] = narrow_loc[...].T
    local[6].wait()
    pair = conv_loc[0].astype(F32)
    second = conv_loc[1].astype(F32)
    third = conv_loc[2].astype(F32)
    fourth = conv_loc[3].astype(F32)
    last = conv_loc[4].astype(F32)

    def put_tap(index, even, odd):
        conv_t[index, 0:OUTS, :] = even.astype(BF).T
        conv_t[index, OUTS : 2 * OUTS, :] = odd.astype(BF).T

    put_tap(0, pair + second, pair)
    put_tap(1, third + fourth, second + third)
    put_tap(2, last, fourth + last)

    for d in range(1, 8):
        landed = half(exit_full, (m + 8 - d) % 8, 1 - core)
        arrive(landed, xf_ss.at[d], xf_rs.at[d])

    def turn_exit(i, _):
        at = pl.ds(pl.multiple_of(i * 256, 256), 256)
        exit_t[at, :] = exit_full[:, at].T
        return 0

    lax.fori_loop(0, D // 256, turn_exit, 0)

    for d in range(1, 8):
        landed = att_full.at[pl.ds(pl.multiple_of(((m + 8 - d) % 8) * 192, 192), 192)]
        arrive(landed, att_ss.at[d], att_rs.at[d])

    def exit_step(i, total):
        at = pl.ds(pl.multiple_of(i * 256, 256), 256)
        tile = (stream_t[at, :].astype(F32) + dot(exit_t[at, :], att_full[...])).astype(BF)
        mixed_t[at, :] = tile
        wide = tile.astype(F32)
        return total + jnp.sum(wide * wide, axis=0, keepdims=True)

    squares = lax.fori_loop(0, D // 256, exit_step, jnp.zeros((1, T), F32))
    second_scale = lax.rsqrt(squares / D + EPS)
    inner = dot(widen_t[...], mixed_t[...]) * second_scale
    inner_t[...] = jnp.maximum(inner, 0.0).astype(BF)

    for d in range(1, 8):
        slice_rows = pl.ds(pl.multiple_of(((m + d) % 8) * 192, 192), 192)
        rs_send[d] = dot(narrow_t[slice_rows, :], inner_t[...]).astype(BF)
        push(rs_send.at[d], rs_recv.at[d], sum_ss.at[d], sum_rs.at[d], mp_peer(d))
    total = mixed_t[my_rows, :].astype(F32) + dot(narrow_t[my_rows, :], inner_t[...])
    for d in range(1, 8):
        arrive(rs_recv.at[d], sum_ss.at[d], sum_rs.at[d])
        total = total + rs_recv[d].astype(F32)
    fin_full[my_rows, :] = total.astype(BF)
    for d in range(1, 8):
        push(
            fin_full.at[my_rows], fin_full.at[my_rows], fin_ss.at[d], fin_rs.at[d], mp_peer(d)
        )
    for d in range(1, 8):
        landed = fin_full.at[pl.ds(pl.multiple_of(((m + 8 - d) % 8) * 192, 192), 192)]
        arrive(landed, fin_ss.at[d], fin_rs.at[d])

    edge_send[0] = dot(conv_t[0], fin_full[:, T - 128 :])
    edge_send[1] = dot(conv_t[2], fin_full[:, :128])
    push(edge_send.at[0], edge_recv.at[0], edge_ss.at[0], edge_rs.at[0], ((s + 1) % 16, m))
    push(edge_send.at[1], edge_recv.at[1], edge_ss.at[1], edge_rs.at[1], ((s + 15) % 16, m))
    before = dot(conv_t[0], fin_full[...])
    here = dot(conv_t[1], fin_full[...])
    after = dot(conv_t[2], fin_full[...])
    arrive(edge_recv.at[0], edge_ss.at[0], edge_rs.at[0])
    arrive(edge_recv.at[1], edge_ss.at[1], edge_rs.at[1])
    left = jnp.where(s > 0, edge_recv[0][:, 127:128], 0.0)
    right = jnp.where(s < 15, edge_recv[1][:, 0:1], 0.0)
    before = jnp.concatenate([left, before[:, : T - 1]], axis=1)
    after = jnp.concatenate([after[:, 1:], right], axis=1)
    result = (before + here + after).astype(BF)
    rows = lax.broadcasted_iota(jnp.int32, (256, 256), 0)
    cols = lax.broadcasted_iota(jnp.int32, (256, 256), 1)
    weave = jnp.where(cols == 2 * (rows % 128) + rows // 128, 1.0, 0.0).astype(BF)
    for b in range(4):
        pair = jnp.concatenate(
            [
                result[:OUTS, b * 128 : (b + 1) * 128],
                result[OUTS:, b * 128 : (b + 1) * 128],
            ],
            axis=1,
        )
        out_ref[:, b * 256 : (b + 1) * 256] = dot(pair, weave).astype(BF)

    for copy in pending:
        copy.wait_send()


def per_device(codes, e, g1, w, sharp, exit_map, g2, widen, narrow, conv):
    any_space = pl.BlockSpec(memory_space=pl.ANY)
    vmem = pl.BlockSpec(memory_space=pltpu.VMEM)
    smem = pl.BlockSpec(memory_space=pltpu.SMEM)
    dma = pltpu.SemaphoreType.DMA((8,))
    return pl.pallas_call(
        kernel,
        out_shape=jax.ShapeDtypeStruct((OUTS, 2 * T), BF),
        in_specs=[
            any_space,
            any_space,
            vmem,
            any_space,
            smem,
            any_space,
            vmem,
            any_space,
            any_space,
            any_space,
        ],
        out_specs=vmem,
        scratch_shapes=[
            pltpu.VMEM((T, PATCH), jnp.int32),
            pltpu.VMEM((8, T, PATCH), BF),
            pltpu.VMEM((T, PATCH), BF),
            pltpu.VMEM((T, 192), BF),
            pltpu.VMEM((D, T), BF),
            pltpu.VMEM((D, 448), BF),
            pltpu.VMEM((T, D), BF),
            pltpu.VMEM((T, T), BF),
            pltpu.VMEM((D, D), BF),
            pltpu.VMEM((D, D), BF),
            pltpu.VMEM((D, T), BF),
            pltpu.VMEM((8, 8, T), F32),
            pltpu.VMEM((8, T), F32),
            pltpu.VMEM((8 * T, PROBE), BF),
            pltpu.VMEM((8 * T, 256), BF),
            pltpu.VMEM((2, T, PROBE), BF),
            pltpu.VMEM((2, T, 256), F32),
            pltpu.VMEM((T, 256), F32),
            pltpu.VMEM((D, T), BF),
            pltpu.VMEM((D, T), BF),
            pltpu.VMEM((D, HIDDEN), BF),
            pltpu.VMEM((HIDDEN, D), BF),
            pltpu.VMEM((HIDDEN, D), BF),
            pltpu.VMEM((D, HIDDEN), BF),
            pltpu.VMEM((HIDDEN, T), BF),
            pltpu.VMEM((8, 192, T), BF),
            pltpu.VMEM((8, 192, T), BF),
            pltpu.VMEM((D, T), BF),
            pltpu.VMEM((5, D, OUTS), BF),
            pltpu.VMEM((3, 2 * OUTS, D), BF),
            pltpu.VMEM((2 * OUTS, T), F32),
            pltpu.VMEM((2, 2 * OUTS, 128), F32),
            pltpu.VMEM((2, 2 * OUTS, 128), F32),
        ]
        + [dma] * 23,
        compiler_params=pltpu.CompilerParams(
            collective_id=0, has_side_effects=True, vmem_limit_bytes=60 * 1024 * 1024
        ),
        cost_estimate=pl.CostEstimate(
            flops=8_000_000_000, bytes_accessed=8_000_000, transcendentals=4_000_000
        ),
        name="genomic_forward",
    )(
        codes.reshape(T, PATCH),
        e,
        g1.reshape(1, D),
        w,
        sharp,
        exit_map,
        g2.reshape(1, D),
        widen,
        narrow,
        conv,
    )


def solution(mesh):
    in_specs = (
        P("seq"),
        P(None, "mp"),
        P(),
        P(None, "mp"),
        P("mp"),
        P("mp", None),
        P(),
        P(None, "mp"),
        P("mp", None),
        P(None, None, "mp"),
    )
    return jax.shard_map(
        per_device, mesh=mesh, in_specs=in_specs, out_specs=P("mp", "seq"), check_vma=False
    )
```

```python
import jax
import jax.numpy as jnp
from jax import lax
from jax.experimental import pallas as pl
from jax.experimental.pallas import tpu as pltpu
from jax.sharding import PartitionSpec as P

MESH = pl.DeviceIdType.MESH
BF = jnp.bfloat16
F32 = jnp.float32

D = 1536
T = 512
PROBE = 128
VALUE = 192
HIDDEN = 384
OUTS = 96
PATCH = 128
EPS = 1e-06
LOG2E = 1.4426950408889634


def dot(a, b):
    return jnp.dot(a, b, preferred_element_type=F32)


def dot_nt(a, b):
    return lax.dot_general(a, b, (((1,), (1,)), ((), ())), preferred_element_type=F32)


def dot_tn(a, b):
    return lax.dot_general(a, b, (((0,), (0,)), ((), ())), preferred_element_type=F32)


def one_hot_codes(codes):
    wide = codes.astype(F32)
    parts = [jnp.where(wide == float(b), 1.0, 0.0).astype(BF) for b in range(4)]
    return jnp.concatenate(parts, axis=1)


def token_columns(row, width):
    high = row.astype(BF)
    low = (row - high.astype(F32)).astype(BF)
    both = jnp.concatenate(
        [jnp.broadcast_to(high, (16, T)), jnp.broadcast_to(low, (16, T))], axis=0
    )
    return dot_tn(both, jnp.full((32, width), 1.0 / 16.0, BF))


def kernel(
    codes_hbm,
    e_hbm,
    g1_ref,
    w_hbm,
    sharp_ref,
    exit_hbm,
    g2_ref,
    widen_hbm,
    narrow_hbm,
    conv_hbm,
    out_ref,
    codes_i,
    codes_all,
    codes_sib,
    e_loc,
    et_full,
    w_loc,
    wg_t,
    m_t,
    exit_full,
    exit_t,
    stream_t,
    u_all,
    u_sib,
    keys,
    vals,
    queries,
    acc,
    part_recv,
    att_send,
    att_full,
    mixed_t,
    widen_loc,
    widen_t,
    narrow_loc,
    narrow_t,
    inner_t,
    rs_sib_send,
    rs_sib,
    rs_send,
    rs_half,
    rs_recv,
    fin_full,
    conv_loc,
    conv_t,
    edge_send,
    edge_recv,
    out_send,
    out_recv,
    in_sem,
    *sems,
):
    pairs = [sems[2 * i : 2 * i + 2] for i in range(17)]
    codes_sems, za_sems, zb_sems, w_sems, e_sems, ef_sems, x_sems, xf_sems = pairs[:8]
    u_sems, p_sems, att_sems, attf_sems, sib_sems, sum_sems, fin_sems, finf_sems = pairs[8:16]
    edge_sems = pairs[16]

    s = lax.axis_index("seq")
    m = lax.axis_index("mp")
    core = s % 2
    j = s // 2
    z = j % 4
    y_lo = j // 4
    x = m % 4
    hi = m // 4
    sib = s + 1 - 2 * core
    m4 = (m + 4) % 8
    s8 = (s + 8) % 16
    native = core == hi
    shard = core * 4 + x

    def send(src, dst, sems, d, dev):
        return pltpu.make_async_remote_copy(
            src_ref=src,
            dst_ref=dst,
            send_sem=sems[0].at[d],
            recv_sem=sems[1].at[d],
            device_id=dev,
            device_id_type=MESH,
        )

    pending = []

    def push(src, dst, sems, d, dev):
        copy = send(src, dst, sems, d, dev)
        copy.start()
        pending.append(copy)

    def arrive(dst, sems, d):
        send(dst, dst, sems, d, (sib, m)).wait_recv()

    class Ring:
        def __init__(self, piece, sems, right, left, other=None, sib_sems=None):
            self.piece, self.sems, self.right, self.left = piece, sems, right, left
            self.other, self.sib_sems = other, sib_sems

        def go(self, block, half, d, dev):
            push(self.piece(block, half), self.piece(block, half), self.sems, d, dev)

        def forward(self, block, half, d):
            if self.sib_sems is not None:
                push(self.piece(block, half), self.piece(block, half), self.sib_sems, d, (sib, m))

        def start(self):
            self.go(0, 0, 0, self.right)
            self.go(0, 1, 1, self.left)
            self.go(0, 1, 2, self.right)
            self.go(0, 0, 3, self.left)
            self.forward(0, 0, 0)
            self.forward(0, 1, 1)

        def relay(self):
            arrive(self.piece(3, 0), self.sems, 0)
            self.go(3, 0, 4, self.right)
            arrive(self.piece(1, 1), self.sems, 1)
            self.go(1, 1, 5, self.left)
            self.forward(3, 0, 2)
            self.forward(1, 1, 3)

        def near(self):
            arrive(self.piece(3, 1), self.sems, 2)
            self.forward(3, 1, 4)
            arrive(self.piece(1, 0), self.sems, 3)
            self.forward(1, 0, 5)

        def opposite(self):
            arrive(self.piece(2, 0), self.sems, 4)
            self.forward(2, 0, 6)
            arrive(self.piece(2, 1), self.sems, 5)
            self.forward(2, 1, 7)

        def others(self):
            for d, (block, half) in enumerate(
                [(0, 0), (0, 1), (3, 0), (1, 1), (3, 1), (1, 0), (2, 0), (2, 1)]
            ):
                arrive(self.other(block, half), self.sib_sems, d)

    def x_ring(ref, ring_sems, forward_sems):
        def of(c):
            def piece(block, half):
                first = (c * 4 + (x + block) % 4) * 192 + half * 96
                return ref.at[pl.ds(pl.multiple_of(first, 96), 96)]

            return piece

        right = (s, hi * 4 + (x + 1) % 4)
        left = (s, hi * 4 + (x + 3) % 4)
        return Ring(of(core), ring_sems, right, left, of(1 - core), forward_sems)

    def z_ring(y, ring_sems):
        def piece(block, half):
            return codes_all.at[y * 4 + (z + block) % 4, pl.ds(half * 256, 256)]

        right = ((y_lo * 4 + (z + 1) % 4) * 2 + core, m)
        left = ((y_lo * 4 + (z + 3) % 4) * 2 + core, m)
        return Ring(piece, ring_sems, right, left)

    def seq_peer(d):
        return (2 * ((j + d) % 8) + core, m)

    def shard_rows(index):
        return pl.ds(pl.multiple_of(index * 192, 192), 192)

    my_rows = shard_rows(shard)

    codes_in = pltpu.make_async_copy(codes_hbm, codes_i, in_sem.at[0])
    codes_in.start()
    w_in = pltpu.make_async_copy(w_hbm, w_loc, in_sem.at[1])
    weights = [
        (e_hbm, e_loc),
        (exit_hbm, exit_full.at[my_rows]),
        (widen_hbm, widen_loc),
        (narrow_hbm, narrow_loc),
        (conv_hbm, conv_loc),
    ]
    weights_in = [
        pltpu.make_async_copy(src, dst, in_sem.at[2 + i]) for i, (src, dst) in enumerate(weights)
    ]
    weights_out = [send(src, dst, w_sems, i, (s8, m4)) for i, (src, dst) in enumerate(weights)]

    @pl.when(native)
    def _():
        weights_in[0].start()

    w_in.start()

    @pl.when(native)
    def _():
        for copy in weights_in[1:]:
            copy.start()

    def weight_here(i):
        @pl.when(native)
        def _():
            weights_in[i].wait()

        @pl.when(jnp.logical_not(native))
        def _():
            weights_out[i].wait_recv()

    barrier = pltpu.get_barrier_semaphore()
    x_e = x_ring(et_full, e_sems, ef_sems)
    x_exit = x_ring(exit_full, x_sems, xf_sems)
    x_att = x_ring(att_full, att_sems, attf_sems)
    x_fin = x_ring(fin_full, fin_sems, finf_sems)
    z_own = z_ring(y_lo, za_sems)
    z_other = z_ring(1 - y_lo, zb_sems)
    far = (s + 14 + 4 * hi) % 16
    greet = [seq_peer(d) for d in range(1, 8)]
    greet += [x_e.right, x_e.left, (sib, m), (s8, m4), (sib, m4), (s, m4), (far, m4)]
    for dev in greet:
        pl.semaphore_signal(barrier, inc=1, device_id=dev, device_id_type=MESH)

    rows = lax.broadcasted_iota(jnp.int32, (T, T), 0)
    cols = lax.broadcasted_iota(jnp.int32, (T, T), 1)
    order = jnp.where(rows == 4 * (cols % PATCH) + cols // PATCH, 1.0, 0.0).astype(BF)
    codes_in.wait()
    codes_all[j] = codes_i[...].astype(BF)
    pl.semaphore_wait(barrier, len(greet))

    @pl.when(native)
    def _():
        for copy in weights_out[:4]:
            copy.start()

    push(codes_all.at[j], codes_all.at[j], codes_sems, 1, (s8, m))
    z_own.start()
    push(codes_all.at[j], codes_sib, codes_sems, 0, (sib, m))
    weight_here(0)
    et_full[my_rows, :] = dot(e_loc[...], order).astype(BF)
    x_e.start()
    z_own.relay()

    w_in.wait()
    gain = g1_ref[...].astype(F32).reshape(1, D)
    wg_t[0:448, :] = (w_loc[...].astype(F32) * gain).astype(BF)
    wg_t[448:512, :] = jnp.zeros((64, D), BF)

    x_e.relay()
    j_other = (1 - y_lo) * 4 + z
    arrive(codes_all.at[j_other], codes_sems, 1)
    z_other.start()
    x_e.near()
    x_e.opposite()
    weight_here(1)
    x_exit.start()
    x_e.others()

    def stream_of(codes):
        hot = one_hot_codes(codes)

        def step(i, total):
            at = pl.ds(pl.multiple_of(i * 256, 256), 256)
            tile = dot_nt(et_full[at, :], hot).astype(BF)
            stream_t[at, :] = tile
            wide = tile.astype(F32)
            return total + jnp.sum(wide * wide, axis=0, keepdims=True)

        return lax.fori_loop(0, D // 256, step, jnp.zeros((1, T), F32))

    u_all[j] = jnp.broadcast_to(stream_of(codes_all[j]) / D + EPS, (8, T))
    push(u_all.at[j], u_sib, u_sems, 0, (sib, m))
    for d in range(1, 8):
        push(u_all.at[j], u_all.at[j], u_sems, d, seq_peer(d))
    z_other.relay()

    m_t[...] = dot(wg_t[...], et_full[...]).astype(BF)

    lanes = lax.broadcasted_iota(jnp.int32, (T, 256), 1)

    def keys_values(block, at):
        hot = one_hot_codes(codes_all[block])
        raw = dot_nt(hot, m_t[128:512, :])
        spread = token_columns(u_all[block][0:1], 128)
        key = raw[:, :128]
        mean = jnp.mean(key * key, axis=1, keepdims=True)
        keys[at, :] = (key * lax.rsqrt(mean + EPS * spread)).astype(BF)
        inverse = lax.rsqrt(spread)
        value = raw[:, 128:] * jnp.concatenate([inverse, inverse], axis=1)
        vals[at, :] = jnp.where(lanes < VALUE, value, 1.0).astype(BF)

    factor = sharp_ref[0] * (LOG2E / PROBE)

    def make_queries(slot, codes, u_row):
        raw = dot_nt(one_hot_codes(codes), m_t[0:128, :])
        spread = token_columns(u_row, 128)
        mean = jnp.mean(raw * raw, axis=1, keepdims=True)
        queries[slot] = (raw * (lax.rsqrt(mean + EPS * spread) * factor)).astype(BF)

    keys_values(j, pl.ds(0, T))
    make_queries(1, codes_all[j], u_all[j][0:1])
    arrive(codes_sib, codes_sems, 0)
    arrive(u_sib, u_sems, 0)
    make_queries(0, codes_sib[...], u_sib[0:1])

    z_own.near()
    z_own.opposite()
    z_other.near()
    z_other.opposite()
    for d in range(1, 8):
        block = (j + 8 - d) % 8
        arrive(u_all.at[block], u_sems, d)
        keys_values(block, pl.ds(d * T, T))

    def attend(slot):
        def chunk(q, _):
            at = pl.ds(pl.multiple_of(q * 256, 256), 256)
            asked = queries[slot, at, :]

            def step(k, total):
                span = pl.ds(pl.multiple_of(k * 1024, 1024), 1024)
                weights = jnp.exp2(dot_nt(asked, keys[span, :])).astype(BF)
                return total + dot(weights, vals[span, :])

            acc[slot, at, :] = lax.fori_loop(0, 4, step, jnp.zeros((256, 256), F32), unroll=True)
            return 0

        lax.fori_loop(0, 2, chunk, 0)

    def attended():
        whole = acc[1] + part_recv[...]
        return (whole[:, :VALUE] / whole[:, VALUE : VALUE + 1]).astype(BF).T

    part = send(acc.at[0], part_recv, p_sems, 0, (sib, m))
    moved = send(att_send, att_full.at[shard_rows(m)], p_sems, 1, (sib, m4))
    slot = jnp.where(native, 0, 1)
    attend(slot)

    @pl.when(native)
    def _():
        part.start()

    x_exit.relay()

    @pl.when(jnp.logical_not(native))
    def _():
        part.wait_recv()
        att_send[...] = attended()
        moved.start()

    attend(1 - slot)

    @pl.when(native)
    def _():
        part.wait_recv()
        att_full[my_rows, :] = attended()

    @pl.when(jnp.logical_not(native))
    def _():
        part.start()
        moved.wait_recv()

    x_att.start()

    weight_here(2)
    gain = g2_ref[...].astype(F32).reshape(1, D)
    widen_t[...] = (widen_loc[...].T.astype(F32) * gain).astype(BF)
    x_exit.near()
    x_exit.opposite()
    x_att.relay()
    x_exit.others()

    @pl.when(native)
    def _():
        weights_out[4].start()

    @pl.when(jnp.logical_not(native))
    def _():
        stream_of(codes_sib[...])

    def turn_exit(i, _):
        at = pl.ds(pl.multiple_of(i * 256, 256), 256)
        exit_t[at, :] = exit_full[:, at].T
        return 0

    lax.fori_loop(0, D // 256, turn_exit, 0)
    x_att.near()
    x_att.opposite()
    x_att.others()

    def exit_step(i, total):
        at = pl.ds(pl.multiple_of(i * 256, 256), 256)
        tile = (stream_t[at, :].astype(F32) + dot(exit_t[at, :], att_full[...])).astype(BF)
        mixed_t[at, :] = tile
        wide = tile.astype(F32)
        return total + jnp.sum(wide * wide, axis=0, keepdims=True)

    squares = lax.fori_loop(0, D // 256, exit_step, jnp.zeros((1, T), F32))
    second_scale = lax.rsqrt(squares / D + EPS)
    inner = dot(widen_t[...], mixed_t[...]) * second_scale
    inner_t[...] = jnp.maximum(inner, 0.0).astype(BF)

    weight_here(3)
    narrow_t[...] = narrow_loc[...].T

    def partial(c, block):
        return dot(narrow_t[shard_rows(c * 4 + (x + block) % 4), :], inner_t[...])

    for block in (2, 1, 3, 0):
        rs_sib_send[block] = partial(1 - core, block).astype(BF)
        push(rs_sib_send.at[block], rs_sib.at[block], sib_sems, block, (sib, m))

    def pair_sum(block):
        mine = partial(core, block)
        arrive(rs_sib.at[block], sib_sems, block)
        return mine + rs_sib[block].astype(F32)

    rs_send[2] = pair_sum(2).astype(BF)
    push(rs_send.at[2, pl.ds(0, 96)], rs_half.at[0], sum_sems, 0, x_fin.right)
    push(rs_send.at[2, pl.ds(96, 96)], rs_half.at[1], sum_sems, 1, x_fin.left)
    right_sum = pair_sum(1)
    left_sum = pair_sum(3)
    arrive(rs_half.at[0], sum_sems, 0)
    rs_send[1, 0:96] = (right_sum[0:96] + rs_half[0].astype(F32)).astype(BF)
    rs_send[1, 96:192] = right_sum[96:192].astype(BF)
    push(rs_send.at[1], rs_recv.at[0], sum_sems, 2, x_fin.right)
    arrive(rs_half.at[1], sum_sems, 1)
    rs_send[3, 0:96] = left_sum[0:96].astype(BF)
    rs_send[3, 96:192] = (left_sum[96:192] + rs_half[1].astype(F32)).astype(BF)
    push(rs_send.at[3], rs_recv.at[1], sum_sems, 3, x_fin.left)
    total = mixed_t[my_rows, :].astype(F32) + pair_sum(0)
    arrive(rs_recv.at[0], sum_sems, 2)
    arrive(rs_recv.at[1], sum_sems, 3)
    fin_full[my_rows, :] = (total + rs_recv[0].astype(F32) + rs_recv[1].astype(F32)).astype(BF)
    x_fin.start()

    weight_here(4)
    first = conv_loc[0].astype(F32)
    second = conv_loc[1].astype(F32)
    third = conv_loc[2].astype(F32)
    fourth = conv_loc[3].astype(F32)
    last = conv_loc[4].astype(F32)

    def put_tap(index, even, odd):
        conv_t[index, 0:OUTS, :] = even.astype(BF)
        conv_t[index, OUTS : 2 * OUTS, :] = odd.astype(BF)

    put_tap(0, first + second, first)
    put_tap(1, third + fourth, second + third)
    put_tap(2, last, fourth + last)

    x_fin.relay()
    x_fin.near()
    x_fin.opposite()
    x_fin.others()

    edge_send[0] = dot(conv_t[0], fin_full[:, T - 128 :])
    edge_send[1] = dot(conv_t[2], fin_full[:, :128])
    push(edge_send.at[0], edge_recv.at[0], edge_sems, 0, ((s + 2 * hi) % 16, m4))
    push(edge_send.at[1], edge_recv.at[1], edge_sems, 1, ((s + 14 + 2 * hi) % 16, m4))
    before = dot(conv_t[0], fin_full[...])
    here = dot(conv_t[1], fin_full[...])
    after = dot(conv_t[2], fin_full[...])
    arrive(edge_recv.at[0], edge_sems, 0)
    arrive(edge_recv.at[1], edge_sems, 1)
    place = 2 * j + hi
    left = jnp.where(place > 0, edge_recv[0][:, 127:128], 0.0)
    right = jnp.where(place < 15, edge_recv[1][:, 0:1], 0.0)
    before = jnp.concatenate([left, before[:, : T - 1]], axis=1)
    after = jnp.concatenate([after[:, 1:], right], axis=1)
    result = (before + here + after).astype(BF)
    rows = lax.broadcasted_iota(jnp.int32, (256, 256), 0)
    cols = lax.broadcasted_iota(jnp.int32, (256, 256), 1)
    weave = jnp.where(cols == 2 * (rows % 128) + rows // 128, 1.0, 0.0).astype(BF)
    for b in range(4):
        pair = jnp.concatenate(
            [
                result[:OUTS, b * 128 : (b + 1) * 128],
                result[OUTS:, b * 128 : (b + 1) * 128],
            ],
            axis=1,
        )
        out_send[:, b * 256 : (b + 1) * 256] = dot(pair, weave).astype(BF)

    placed = send(out_send, out_recv, edge_sems, 2, (sib, m4))

    @pl.when(native)
    def _():
        out_ref[...] = out_send[...]

    @pl.when(jnp.logical_not(native))
    def _():
        placed.start()
        placed.wait_recv()
        out_ref[...] = out_recv[...]

    part.wait_send()

    @pl.when(native)
    def _():
        for copy in weights_out:
            copy.wait_send()

    @pl.when(jnp.logical_not(native))
    def _():
        moved.wait_send()
        placed.wait_send()

    for copy in pending:
        copy.wait_send()


def per_device(codes, e, g1, w, sharp, exit_map, g2, widen, narrow, conv):
    any_space = pl.BlockSpec(memory_space=pl.ANY)
    vmem = pl.BlockSpec(memory_space=pltpu.VMEM)
    smem = pl.BlockSpec(memory_space=pltpu.SMEM)
    dma = pltpu.SemaphoreType.DMA((8,))
    return pl.pallas_call(
        kernel,
        out_shape=jax.ShapeDtypeStruct((OUTS, 2 * T), BF),
        in_specs=[
            any_space,
            any_space,
            vmem,
            any_space,
            smem,
            any_space,
            vmem,
            any_space,
            any_space,
            any_space,
        ],
        out_specs=vmem,
        scratch_shapes=[
            pltpu.VMEM((T, PATCH), jnp.int32),
            pltpu.VMEM((8, T, PATCH), BF),
            pltpu.VMEM((T, PATCH), BF),
            pltpu.VMEM((192, T), BF),
            pltpu.VMEM((D, T), BF),
            pltpu.VMEM((448, D), BF),
            pltpu.VMEM((T, D), BF),
            pltpu.VMEM((T, T), BF),
            pltpu.VMEM((D, D), BF),
            pltpu.VMEM((D, D), BF),
            pltpu.VMEM((D, T), BF),
            pltpu.VMEM((8, 8, T), F32),
            pltpu.VMEM((8, T), F32),
            pltpu.VMEM((8 * T, PROBE), BF),
            pltpu.VMEM((8 * T, 256), BF),
            pltpu.VMEM((2, T, PROBE), BF),
            pltpu.VMEM((2, T, 256), F32),
            pltpu.VMEM((T, 256), F32),
            pltpu.VMEM((192, T), BF),
            pltpu.VMEM((D, T), BF),
            pltpu.VMEM((D, T), BF),
            pltpu.VMEM((D, HIDDEN), BF),
            pltpu.VMEM((HIDDEN, D), BF),
            pltpu.VMEM((HIDDEN, D), BF),
            pltpu.VMEM((D, HIDDEN), BF),
            pltpu.VMEM((HIDDEN, T), BF),
            pltpu.VMEM((4, 192, T), BF),
            pltpu.VMEM((4, 192, T), BF),
            pltpu.VMEM((4, 192, T), BF),
            pltpu.VMEM((2, 96, T), BF),
            pltpu.VMEM((2, 192, T), BF),
            pltpu.VMEM((D, T), BF),
            pltpu.VMEM((5, OUTS, D), BF),
            pltpu.VMEM((3, 2 * OUTS, D), BF),
            pltpu.VMEM((2, 2 * OUTS, 128), F32),
            pltpu.VMEM((2, 2 * OUTS, 128), F32),
            pltpu.VMEM((OUTS, 2 * T), BF),
            pltpu.VMEM((OUTS, 2 * T), BF),
        ]
        + [dma] * 35,
        compiler_params=pltpu.CompilerParams(
            collective_id=0, has_side_effects=True, vmem_limit_bytes=60 * 1024 * 1024
        ),
        cost_estimate=pl.CostEstimate(
            flops=8_000_000_000, bytes_accessed=8_000_000, transcendentals=4_000_000
        ),
        name="genomic_forward",
    )(
        codes.reshape(T, PATCH),
        e.T,
        g1,
        w.T,
        sharp,
        exit_map,
        g2,
        widen,
        narrow,
        conv.transpose(0, 2, 1),
    )


def solution(mesh):
    in_specs = (
        P("seq"),
        P(None, "mp"),
        P(),
        P(None, "mp"),
        P("mp"),
        P("mp", None),
        P(),
        P(None, "mp"),
        P("mp", None),
        P(None, None, "mp"),
    )
    return jax.shard_map(
        per_device, mesh=mesh, in_specs=in_specs, out_specs=P("mp", "seq"), check_vma=False
    )
```

```python
import jax
import jax.numpy as jnp
from jax import lax
from jax.experimental import pallas as pl
from jax.experimental.pallas import tpu as pltpu
from jax.sharding import PartitionSpec as P

MESH = pl.DeviceIdType.MESH
BF = jnp.bfloat16
F32 = jnp.float32

D = 1536
T = 512
TH = 256
PROBE = 128
VALUE = 192
HIDDEN = 384
OUTS = 96
PATCH = 128
EPS = 1e-06
LOG2E = 1.4426950408889634


def dot(a, b):
    return jnp.dot(a, b, preferred_element_type=F32)


def dot_nt(a, b):
    return lax.dot_general(a, b, (((1,), (1,)), ((), ())), preferred_element_type=F32)


def dot_tn(a, b):
    return lax.dot_general(a, b, (((0,), (0,)), ((), ())), preferred_element_type=F32)


def one_hot_codes(codes):
    wide = codes.astype(F32)
    parts = [jnp.where(wide == float(b), 1.0, 0.0).astype(BF) for b in range(4)]
    return jnp.concatenate(parts, axis=1)


def token_columns(row, width):
    high = row.astype(BF)
    low = (row - high.astype(F32)).astype(BF)
    both = jnp.concatenate(
        [jnp.broadcast_to(high, (16, T)), jnp.broadcast_to(low, (16, T))], axis=0
    )
    return dot_tn(both, jnp.full((32, width), 1.0 / 16.0, BF))


def kernel(
    codes_hbm,
    e_hbm,
    g1_ref,
    w_hbm,
    sharp_ref,
    exit_hbm,
    g2_ref,
    widen_hbm,
    narrow_hbm,
    conv_hbm,
    out_ref,
    codes_i,
    codes_all,
    codes_sib,
    e_loc,
    et_full,
    w_loc,
    wg_t,
    m_t,
    exit_full,
    stream,
    u_all,
    u_sib,
    keys,
    vals,
    queries,
    part_send,
    part_recv,
    att_send,
    att_full,
    att,
    mixed,
    widen_all,
    narrow_loc,
    narrow_t,
    rs_send,
    rs_half,
    rs_recv,
    fin_full,
    conv_all,
    conv_t,
    edge_send,
    edge_recv,
    out_send,
    out_recv,
    in_sem,
    *sems,
):
    pairs = [sems[2 * i : 2 * i + 2] for i in range(15)]
    codes_sems, za_sems, zb_sems, w_sems, wf_sems, e_sems, ef_sems, x_sems = pairs[:8]
    xf_sems, u_sems, p_sems, att_sems, sum_sems, fin_sems, edge_sems = pairs[8:]

    s = lax.axis_index("seq")
    m = lax.axis_index("mp")
    core = s % 2
    j = s // 2
    z = j % 4
    y_lo = j // 4
    x = m % 4
    hi = m // 4
    sib = s + 1 - 2 * core
    m4 = (m + 4) % 8
    s8 = (s + 8) % 16

    def send(src, dst, sems, d, dev):
        return pltpu.make_async_remote_copy(
            src_ref=src,
            dst_ref=dst,
            send_sem=sems[0].at[d],
            recv_sem=sems[1].at[d],
            device_id=dev,
            device_id_type=MESH,
        )

    pending = []

    def push(src, dst, sems, d, dev):
        copy = send(src, dst, sems, d, dev)
        copy.start()
        pending.append(copy)

    def arrive(dst, sems, d):
        send(dst, dst, sems, d, (sib, m)).wait_recv()

    class Ring:
        def __init__(self, piece, sems, right, left, other=None, sib_sems=None):
            self.piece, self.sems, self.right, self.left = piece, sems, right, left
            self.other, self.sib_sems = other, sib_sems

        def go(self, block, which, d, dev):
            push(self.piece(block, which), self.piece(block, which), self.sems, d, dev)

        def forward(self, block, which, d):
            if self.sib_sems is not None:
                piece = self.piece(block, which)
                push(piece, piece, self.sib_sems, d, (sib, m))

        def start(self, which):
            if which == 0:
                self.go(0, 0, 0, self.right)
                self.go(0, 0, 3, self.left)
            else:
                self.go(0, 1, 1, self.left)
                self.go(0, 1, 2, self.right)
                self.forward(0, 1, 0)

        def relay(self):
            arrive(self.piece(3, 0), self.sems, 0)
            self.go(3, 0, 4, self.right)
            self.forward(3, 0, 1)
            arrive(self.piece(1, 1), self.sems, 1)
            self.go(1, 1, 5, self.left)
            self.forward(1, 1, 2)

        def near(self):
            arrive(self.piece(1, 0), self.sems, 3)
            self.forward(1, 0, 3)
            arrive(self.piece(3, 1), self.sems, 2)
            self.forward(3, 1, 4)

        def opposite(self):
            arrive(self.piece(2, 0), self.sems, 4)
            self.forward(2, 0, 5)
            arrive(self.piece(2, 1), self.sems, 5)
            self.forward(2, 1, 6)

        def others(self):
            order = [(0, 1), (3, 0), (1, 1), (1, 0), (3, 1), (2, 0), (2, 1)]
            for d, (block, which) in enumerate(order):
                arrive(self.other(block, which), self.sib_sems, d)

    right = (s, hi * 4 + (x + 1) % 4)
    left = (s, hi * 4 + (x + 3) % 4)

    def shard(block, which):
        h = hi if which == 0 else 1 - hi
        return h * 4 + (x + block) % 4

    def shard_rows(block, which):
        return pl.ds(pl.multiple_of(shard(block, which) * 192, 192), 192)

    def whole_ring(ref, ring_sems):
        return Ring(lambda block, which: ref.at[shard_rows(block, which)], ring_sems, right, left)

    def half_ring(ref, ring_sems, sib_sems):
        def of(c):
            def piece(block, which):
                first = shard(block, which) * 192 + c * 96
                return ref.at[pl.ds(pl.multiple_of(first, 96), 96)]

            return piece

        return Ring(of(core), ring_sems, right, left, of(1 - core), sib_sems)

    def z_ring(y, ring_sems):
        def piece(block, which):
            return codes_all.at[y * 4 + (z + block) % 4, pl.ds(which * 256, 256)]

        ahead = ((y_lo * 4 + (z + 1) % 4) * 2 + core, m)
        behind = ((y_lo * 4 + (z + 3) % 4) * 2 + core, m)
        return Ring(piece, ring_sems, ahead, behind)

    def seq_peer(d):
        return (2 * ((j + d) % 8) + core, m)

    my_rows = shard_rows(0, 0)
    own_half = pl.ds(pl.multiple_of(core * 96, 96), 96)
    widen_half = pl.ds(pl.multiple_of(core * 768, 768), 768)
    conv_half = pl.ds(pl.multiple_of(core * 48, 48), 48)
    other_widen_half = pl.ds(pl.multiple_of((1 - core) * 768, 768), 768)
    other_conv_half = pl.ds(pl.multiple_of((1 - core) * 48, 48), 48)

    local = [
        pltpu.make_async_copy(src, dst, in_sem.at[i])
        for i, (src, dst) in enumerate(
            [
                (codes_hbm, codes_i),
                (e_hbm, e_loc),
                (w_hbm, w_loc),
                (exit_hbm, exit_full.at[my_rows]),
                (narrow_hbm, narrow_loc),
                (widen_hbm, widen_all.at[hi]),
                (conv_hbm, conv_all.at[hi]),
            ]
        )
    ]
    for copy in local:
        copy.start()

    x_e = half_ring(et_full, e_sems, ef_sems)
    x_exit = half_ring(exit_full, x_sems, xf_sems)
    x_att = whole_ring(att_full, att_sems)
    x_fin = whole_ring(fin_full, fin_sems)
    z_own = z_ring(y_lo, za_sems)
    z_other = z_ring(1 - y_lo, zb_sems)

    barrier = pltpu.get_barrier_semaphore()
    greet = [(sib, m), right, left, (s8, m4), (s8, m), z_own.right, z_own.left]
    for dev in greet:
        pl.semaphore_signal(barrier, inc=1, device_id=dev, device_id_type=MESH)

    rows = lax.broadcasted_iota(jnp.int32, (T, T), 0)
    cols = lax.broadcasted_iota(jnp.int32, (T, T), 1)
    order = jnp.where(rows == 4 * (cols % PATCH) + cols // PATCH, 1.0, 0.0).astype(BF)
    local[0].wait()
    codes_all[j] = codes_i[...].astype(BF)
    local[1].wait()
    et_full[my_rows, :] = dot(e_loc[...], order).astype(BF)

    local[2].wait()
    gain = g1_ref[...].astype(F32).reshape(1, D)
    wg_t[0:448, :] = (w_loc[...].astype(F32) * gain).astype(BF)
    wg_t[448:512, :] = jnp.zeros((64, D), BF)

    pl.semaphore_wait(barrier, len(greet))

    x_e.start(0)
    push(x_e.piece(0, 0), x_e.piece(0, 0), w_sems, 0, (s8, m4))
    push(codes_all.at[j], codes_all.at[j], codes_sems, 1, (s8, m))
    z_own.start(0)
    z_own.start(1)
    push(codes_all.at[j], codes_sib, codes_sems, 0, (sib, m))
    push(exit_hbm.at[own_half], x_exit.piece(0, 0), w_sems, 1, (s8, m4))
    push(widen_hbm.at[widen_half], widen_all.at[hi, widen_half], w_sems, 2, (s8, m4))

    arrive(x_e.piece(0, 1), w_sems, 0)
    x_e.start(1)
    z_own.relay()
    x_e.relay()
    arrive(codes_all.at[(1 - y_lo) * 4 + z], codes_sems, 1)
    z_other.start(0)
    z_other.start(1)
    local[4].wait()
    narrow_t[hi] = narrow_loc[...].T
    mine = narrow_t.at[hi, widen_half]
    push(mine, mine, w_sems, 3, (s8, m4))
    x_e.near()
    x_e.opposite()
    local[3].wait()
    x_exit.start(0)
    z_other.relay()
    x_e.others()
    arrive(x_exit.piece(0, 1), w_sems, 1)
    x_exit.start(1)

    def stream_step(hot):
        def step(i, total):
            at = pl.ds(pl.multiple_of(i * 256, 256), 256)
            wide = dot_nt(et_full[at, :], hot).astype(BF).astype(F32)
            return total + jnp.sum(wide * wide, axis=0, keepdims=True)

        return step

    squares = lax.fori_loop(
        0, D // 256, stream_step(one_hot_codes(codes_all[j])), jnp.zeros((1, T), F32)
    )
    u_all[j] = jnp.broadcast_to(squares / D + EPS, (8, T))
    push(u_all.at[j], u_sib, u_sems, 0, (sib, m))
    z_own.near()
    z_own.opposite()
    z_other.near()
    z_other.opposite()
    for d in range(1, 8):
        push(u_all.at[j], u_all.at[j], u_sems, d, seq_peer(d))

    m_t[...] = dot(wg_t[...], et_full[...]).astype(BF)

    lanes = lax.broadcasted_iota(jnp.int32, (T, 256), 1)

    def keys_values(block, at):
        hot = one_hot_codes(codes_all[block])
        raw = dot_nt(hot, m_t[128:512, :])
        spread = token_columns(u_all[block][0:1], 128)
        key = raw[:, :128]
        mean = jnp.mean(key * key, axis=1, keepdims=True)
        keys[at, :] = (key * lax.rsqrt(mean + EPS * spread)).astype(BF)
        inverse = lax.rsqrt(spread)
        value = raw[:, 128:] * jnp.concatenate([inverse, inverse], axis=1)
        vals[at, :] = jnp.where(lanes < VALUE, value, 1.0).astype(BF)

    factor = sharp_ref[0] * (LOG2E / PROBE)

    def make_queries(slot, codes, u_row):
        raw = dot_nt(one_hot_codes(codes), m_t[0:128, :])
        spread = token_columns(u_row, 128)
        mean = jnp.mean(raw * raw, axis=1, keepdims=True)
        queries[slot] = (raw * (lax.rsqrt(mean + EPS * spread) * factor)).astype(BF)

    keys_values(j, pl.ds(0, T))
    make_queries(core, codes_all[j], u_all[j][0:1])
    arrive(codes_sib, codes_sems, 0)
    arrive(u_sib, u_sems, 0)
    make_queries(1 - core, codes_sib[...], u_sib[0:1])
    for d in range(1, 8):
        block = (j + 8 - d) % 8
        arrive(u_all.at[block], u_sems, d)
        keys_values(block, pl.ds(d * T, T))

    def attend(slot, half):
        asked = queries[slot, pl.ds(pl.multiple_of(half * TH, TH), TH), :]

        def step(k, total):
            span = pl.ds(pl.multiple_of(k * 1024, 1024), 1024)
            weights = jnp.exp2(dot_nt(asked, keys[span, :])).astype(BF)
            return total + dot(weights, vals[span, :])

        return lax.fori_loop(0, 4, step, jnp.zeros((TH, 256), F32), unroll=True)

    def exchange(slot, which):
        part_send[which] = attend(slot, 1 - core)
        push(part_send.at[which], part_recv.at[which], p_sems, which, (sib, m))

    def attended(slot, which):
        whole = attend(slot, core)
        arrive(part_recv.at[which], p_sems, which)
        whole = whole + part_recv[which]
        return (whole[:, :VALUE] / whole[:, VALUE : VALUE + 1]).astype(BF).T

    exchange(1 - hi, 1)
    att_send[...] = attended(1 - hi, 1)
    push(att_send, att_full.at[my_rows], p_sems, 2, (s, m4))
    x_exit.relay()
    exchange(hi, 0)
    arrive(att_full.at[shard_rows(0, 1)], p_sems, 2)
    x_att.start(1)
    x_exit.near()
    att_full[my_rows, :] = attended(hi, 0)
    x_att.start(0)

    foreign_widen = widen_all.at[1 - hi, widen_half]
    arrive(foreign_widen, w_sems, 2)
    push(foreign_widen, foreign_widen, wf_sems, 0, (sib, m))
    x_exit.opposite()
    x_att.relay()

    def group_stream(codes):
        hot = one_hot_codes(codes)

        def step(i, _):
            at = pl.ds(pl.multiple_of(i * 256, 256), 256)
            stream[:, at] = dot_nt(hot, et_full[at, :]).astype(BF)
            return 0

        lax.fori_loop(0, D // 256, step, 0)

    half_rows = pl.ds(pl.multiple_of(core * TH, TH), TH)

    @pl.when(core == hi)
    def _():
        group_stream(codes_all[j, half_rows])

    @pl.when(core != hi)
    def _():
        group_stream(codes_sib[half_rows, :])

    foreign_narrow = narrow_t.at[1 - hi, widen_half]
    arrive(foreign_narrow, w_sems, 3)
    push(foreign_narrow, foreign_narrow, wf_sems, 1, (sib, m))
    x_exit.others()
    push(
        conv_hbm.at[:, conv_half], conv_all.at[hi, :, conv_half], w_sems, 4, (s8, m4)
    )
    x_att.near()
    x_att.opposite()
    for b in range(4):
        att[:, b * 384 : (b + 1) * 384] = att_full[b * 384 : (b + 1) * 384, :].T

    def exit_step(i, total):
        at = pl.ds(pl.multiple_of(i * 256, 256), 256)
        tile = (stream[:, at].astype(F32) + dot(att[...], exit_full[:, at])).astype(BF)
        mixed[:, at] = tile
        wide = tile.astype(F32)
        return total + jnp.sum(wide * wide, axis=1, keepdims=True)

    squares = lax.fori_loop(0, D // 256, exit_step, jnp.zeros((TH, 1), F32))
    second_scale = lax.rsqrt(squares / D + EPS)
    gain = g2_ref[...].astype(F32).reshape(1, D)
    scaled = (mixed[...].astype(F32) * gain).astype(BF)
    local[5].wait()
    arrive(widen_all.at[1 - hi, other_widen_half], wf_sems, 0)
    inner = [
        jnp.maximum(dot(scaled, widen_all[h]) * second_scale, 0.0).astype(BF) for h in range(2)
    ]

    arrive(narrow_t.at[1 - hi, other_widen_half], wf_sems, 1)

    def partial(block, which):
        at = shard_rows(block, which)
        return dot_nt(narrow_t[0, at, :], inner[0]) + dot_nt(narrow_t[1, at, :], inner[1])

    def give(index, value, dst, d, dev):
        rs_send[index] = value.astype(BF)
        push(rs_send.at[index], dst, sum_sems, d, dev)

    give(0, partial(2, 0), rs_half.at[0], 0, right)
    give(1, partial(2, 1), rs_half.at[1], 1, left)
    give(2, partial(1, 1), rs_recv.at[0, 1], 2, right)
    give(3, partial(3, 0), rs_recv.at[1, 0], 3, left)
    right_sum = partial(1, 0)
    left_sum = partial(3, 1)
    arrive(rs_half.at[0], sum_sems, 0)
    give(4, right_sum + rs_half[0].astype(F32), rs_recv.at[0, 0], 4, right)
    arrive(rs_half.at[1], sum_sems, 1)
    give(5, left_sum + rs_half[1].astype(F32), rs_recv.at[1, 1], 5, left)

    def finish(which, from_left, from_right):
        shifted = lax.broadcasted_iota(jnp.int32, (192, D), 0) + shard(0, which) * 192
        pick = jnp.where(lax.broadcasted_iota(jnp.int32, (192, D), 1) == shifted, 1.0, 0.0)
        total = partial(0, which) + dot_nt(pick.astype(BF), mixed[...])
        arrive(rs_recv.at[0, which], sum_sems, from_left)
        arrive(rs_recv.at[1, which], sum_sems, from_right)
        total = total + rs_recv[0, which].astype(F32) + rs_recv[1, which].astype(F32)
        fin_full[shard_rows(0, which), :] = total.astype(BF)
        x_fin.start(which)

    finish(0, 4, 3)
    finish(1, 2, 5)

    foreign_conv = conv_all.at[1 - hi, :, conv_half]
    arrive(foreign_conv, w_sems, 4)
    push(foreign_conv, foreign_conv, wf_sems, 2, (sib, m))
    x_fin.relay()
    local[6].wait()
    arrive(conv_all.at[1 - hi, :, other_conv_half], wf_sems, 2)
    for h in range(2):
        taps = [conv_all[h, k].astype(F32) for k in range(5)]
        folded = [
            (taps[0] + taps[1], taps[0]),
            (taps[2] + taps[3], taps[1] + taps[2]),
            (taps[4], taps[3] + taps[4]),
        ]
        for index, (even, odd) in enumerate(folded):
            conv_t[index, h * 192 : h * 192 + OUTS, :] = even.astype(BF)
            conv_t[index, h * 192 + OUTS : (h + 1) * 192, :] = odd.astype(BF)

    x_fin.near()
    x_fin.opposite()

    edge_send[0] = dot(conv_t[0], fin_full[:, TH - 128 :]).astype(BF)
    edge_send[1] = dot(conv_t[2], fin_full[:, :128]).astype(BF)
    next_s = (s + 16 + (1 - core) + core * (2 * hi - 1)) % 16
    prev_s = (s + 16 - core + (1 - core) * (2 * hi - 1)) % 16
    push(edge_send.at[0], edge_recv.at[0], edge_sems, 0, (next_s, (m + 4 * core) % 8))
    push(edge_send.at[1], edge_recv.at[1], edge_sems, 1, (prev_s, (m + 4 - 4 * core) % 8))
    place = 4 * j + 2 * hi + core
    rows = lax.broadcasted_iota(jnp.int32, (256, 256), 0)
    cols = lax.broadcasted_iota(jnp.int32, (256, 256), 1)
    weave = jnp.where(cols == 2 * (rows % 128) + rows // 128, 1.0, 0.0).astype(BF)

    def taps_of(which):
        h = hi if which == 0 else 1 - hi
        at = pl.ds(pl.multiple_of(h * 192, 192), 192)
        return at, [dot(conv_t[k, at, :], fin_full[...]) for k in range(3)]

    def outputs(at, products):
        before, here, after = products
        left_edge = jnp.where(place > 0, edge_recv[0, at, :][:, 127:128].astype(F32), 0.0)
        right_edge = jnp.where(place < 31, edge_recv[1, at, :][:, 0:1].astype(F32), 0.0)
        before = jnp.concatenate([left_edge, before[:, : TH - 1]], axis=1)
        after = jnp.concatenate([after[:, 1:], right_edge], axis=1)
        result = (before + here + after).astype(BF)
        woven = []
        for b in range(2):
            span = slice(b * 128, (b + 1) * 128)
            both = jnp.concatenate([result[:OUTS, span], result[OUTS:, span]], axis=1)
            woven.append(dot(both, weave).astype(BF))
        return jnp.concatenate(woven, axis=1)

    foreign = taps_of(1)
    arrive(edge_recv.at[0], edge_sems, 0)
    arrive(edge_recv.at[1], edge_sems, 1)
    out_send[1] = outputs(*foreign)
    push(out_send.at[1], out_recv.at[core], edge_sems, 4 + core, (2 * j + hi, m4))
    mine = outputs(*taps_of(0))
    out_send[0] = mine
    to_sibling = send(out_send.at[0], out_recv.at[core], edge_sems, 2 + core, (sib, m))

    @pl.when(core == hi)
    def _():
        out_ref[:, pl.ds(pl.multiple_of(core * T, T), T)] = mine
        arrive(out_recv.at[1 - core], edge_sems, 3 - core)
        out_ref[:, pl.ds(pl.multiple_of((1 - core) * T, T), T)] = out_recv[1 - core]

    @pl.when(core != hi)
    def _():
        to_sibling.start()
        arrive(out_recv.at[0], edge_sems, 4)
        arrive(out_recv.at[1], edge_sems, 5)
        out_ref[:, :T] = out_recv[0]
        out_ref[:, T:] = out_recv[1]
        to_sibling.wait_send()

    for copy in pending:
        copy.wait_send()


def per_device(codes, e, g1, w, sharp, exit_map, g2, widen, narrow, conv):
    any_space = pl.BlockSpec(memory_space=pl.ANY)
    vmem = pl.BlockSpec(memory_space=pltpu.VMEM)
    smem = pl.BlockSpec(memory_space=pltpu.SMEM)
    dma = pltpu.SemaphoreType.DMA((8,))
    return pl.pallas_call(
        kernel,
        out_shape=jax.ShapeDtypeStruct((OUTS, 2 * T), BF),
        in_specs=[
            any_space,
            any_space,
            vmem,
            any_space,
            smem,
            any_space,
            vmem,
            any_space,
            any_space,
            any_space,
        ],
        out_specs=vmem,
        scratch_shapes=[
            pltpu.VMEM((T, PATCH), jnp.int32),
            pltpu.VMEM((8, T, PATCH), BF),
            pltpu.VMEM((T, PATCH), BF),
            pltpu.VMEM((192, T), BF),
            pltpu.VMEM((D, T), BF),
            pltpu.VMEM((448, D), BF),
            pltpu.VMEM((T, D), BF),
            pltpu.VMEM((T, T), BF),
            pltpu.VMEM((D, D), BF),
            pltpu.VMEM((TH, D), BF),
            pltpu.VMEM((8, 8, T), F32),
            pltpu.VMEM((8, T), F32),
            pltpu.VMEM((8 * T, PROBE), BF),
            pltpu.VMEM((8 * T, 256), BF),
            pltpu.VMEM((2, T, PROBE), BF),
            pltpu.VMEM((2, TH, 256), F32),
            pltpu.VMEM((2, TH, 256), F32),
            pltpu.VMEM((192, TH), BF),
            pltpu.VMEM((D, TH), BF),
            pltpu.VMEM((TH, D), BF),
            pltpu.VMEM((TH, D), BF),
            pltpu.VMEM((2, D, HIDDEN), BF),
            pltpu.VMEM((HIDDEN, D), BF),
            pltpu.VMEM((2, D, HIDDEN), BF),
            pltpu.VMEM((6, 192, TH), BF),
            pltpu.VMEM((2, 192, TH), BF),
            pltpu.VMEM((2, 2, 192, TH), BF),
            pltpu.VMEM((D, TH), BF),
            pltpu.VMEM((2, 5, OUTS, D), BF),
            pltpu.VMEM((3, 4 * OUTS, D), BF),
            pltpu.VMEM((2, 4 * OUTS, 128), BF),
            pltpu.VMEM((2, 4 * OUTS, 128), BF),
            pltpu.VMEM((2, OUTS, T), BF),
            pltpu.VMEM((2, OUTS, T), BF),
        ]
        + [dma] * 31,
        compiler_params=pltpu.CompilerParams(
            collective_id=0, has_side_effects=True, vmem_limit_bytes=60 * 1024 * 1024
        ),
        cost_estimate=pl.CostEstimate(
            flops=8_000_000_000, bytes_accessed=8_000_000, transcendentals=4_000_000
        ),
        name="genomic_forward",
    )(
        codes.reshape(T, PATCH),
        e.T,
        g1,
        w.T,
        sharp,
        exit_map,
        g2,
        widen,
        narrow,
        conv.transpose(0, 2, 1),
    )


def solution(mesh):
    in_specs = (
        P("seq"),
        P(None, "mp"),
        P(),
        P(None, "mp"),
        P("mp"),
        P("mp", None),
        P(),
        P(None, "mp"),
        P("mp", None),
        P(None, None, "mp"),
    )
    return jax.shard_map(
        per_device, mesh=mesh, in_specs=in_specs, out_specs=P("mp", "seq"), check_vma=False
    )
```

```python
import jax
import jax.numpy as jnp
from jax import lax
from jax.experimental import pallas as pl
from jax.experimental.pallas import tpu as pltpu
from jax.sharding import PartitionSpec as P

MESH = pl.DeviceIdType.MESH
BF = jnp.bfloat16
F32 = jnp.float32

D = 1536
T = 512
TH = 256
PROBE = 128
VALUE = 192
HIDDEN = 384
OUTS = 96
PATCH = 128
EPS = 1e-06
LOG2E = 1.4426950408889634


def dot(a, b):
    return jnp.dot(a, b, preferred_element_type=F32)


def dot_nt(a, b):
    return lax.dot_general(a, b, (((1,), (1,)), ((), ())), preferred_element_type=F32)


def dot_tn(a, b):
    return lax.dot_general(a, b, (((0,), (0,)), ((), ())), preferred_element_type=F32)


def one_hot_codes(codes):
    wide = codes.astype(F32)
    parts = [jnp.where(wide == float(b), 1.0, 0.0).astype(BF) for b in range(4)]
    return jnp.concatenate(parts, axis=1)


def token_columns(row, width):
    high = row.astype(BF)
    low = (row - high.astype(F32)).astype(BF)
    both = jnp.concatenate(
        [jnp.broadcast_to(high, (16, T)), jnp.broadcast_to(low, (16, T))], axis=0
    )
    return dot_tn(both, jnp.full((32, width), 1.0 / 16.0, BF))


def kernel(
    codes_hbm,
    e_hbm,
    g1_ref,
    w_hbm,
    sharp_ref,
    exit_hbm,
    g2_ref,
    widen_hbm,
    narrow_hbm,
    conv_hbm,
    out_ref,
    codes_i,
    codes_all,
    codes_sib,
    e_loc,
    et_full,
    w_loc,
    wg_t,
    m_t,
    exit_full,
    stream,
    sq_all,
    u_all,
    u_sib,
    keys,
    vals,
    queries,
    part_send,
    part_recv,
    att_send,
    att_full,
    att,
    mixed,
    mixed_t,
    widen_all,
    narrow_loc,
    narrow_t,
    inner_t,
    rs_send,
    rs_half,
    rs_recv,
    fin_full,
    conv_all,
    conv_t,
    halo_send,
    halo_recv,
    edges,
    out_send,
    out_recv,
    in_sem,
    *sems,
):
    pairs = [sems[2 * i : 2 * i + 2] for i in range(15)]
    codes_sems, w_sems, wf_sems, e_sems, ef_sems, x_sems = pairs[:6]
    xf_sems, u_sems, p_sems, att_sems, sum_sems, fin_sems, edge_sems, sq_sems = pairs[6:14]
    out_sems = pairs[14]

    s = lax.axis_index("seq")
    m = lax.axis_index("mp")
    core = s % 2
    j = s // 2
    z = j % 4
    y_lo = j // 4
    x = m % 4
    hi = m // 4
    sib = s + 1 - 2 * core
    m4 = (m + 4) % 8
    s8 = (s + 8) % 16

    def send(src, dst, sems, d, dev):
        return pltpu.make_async_remote_copy(
            src_ref=src,
            dst_ref=dst,
            send_sem=sems[0].at[d],
            recv_sem=sems[1].at[d],
            device_id=dev,
            device_id_type=MESH,
        )

    pending = []

    def push(src, dst, sems, d, dev):
        copy = send(src, dst, sems, d, dev)
        copy.start()
        pending.append(copy)

    def arrive(dst, sems, d):
        send(dst, dst, sems, d, (sib, m)).wait_recv()

    class Ring:
        def __init__(self, piece, sems, right, left, other=None, sib_sems=None):
            self.piece, self.sems, self.right, self.left = piece, sems, right, left
            self.other, self.sib_sems = other, sib_sems

        def go(self, block, which, d, dev):
            push(self.piece(block, which), self.piece(block, which), self.sems, d, dev)

        def forward(self, block, which, d):
            if self.sib_sems is not None:
                piece = self.piece(block, which)
                push(piece, piece, self.sib_sems, d, (sib, m))

        def start(self, which):
            if which == 0:
                self.go(0, 0, 0, self.right)
                self.go(0, 0, 3, self.left)
            else:
                self.go(0, 1, 1, self.left)
                self.go(0, 1, 2, self.right)
                self.forward(0, 1, 0)

        def relay(self, which):
            if which == 0:
                arrive(self.piece(3, 0), self.sems, 0)
                self.go(3, 0, 4, self.right)
                self.forward(3, 0, 1)
            else:
                arrive(self.piece(1, 1), self.sems, 1)
                self.go(1, 1, 5, self.left)
                self.forward(1, 1, 2)

        def near(self):
            arrive(self.piece(1, 0), self.sems, 3)
            self.forward(1, 0, 3)
            arrive(self.piece(3, 1), self.sems, 2)
            self.forward(3, 1, 4)

        def opposite(self):
            arrive(self.piece(2, 0), self.sems, 4)
            self.forward(2, 0, 5)
            arrive(self.piece(2, 1), self.sems, 5)
            self.forward(2, 1, 6)

        def others(self):
            order = [(0, 1), (3, 0), (1, 1), (1, 0), (3, 1), (2, 0), (2, 1)]
            for d, (block, which) in enumerate(order):
                arrive(self.other(block, which), self.sib_sems, d)

    class Direct(Ring):
        def start(self, which):
            across = (s, hi * 4 + (x + 2) % 4)
            for k, dev in enumerate((self.right, self.left, across)):
                self.go(0, which, 3 * which + k, dev)
            if which == 1:
                self.forward(0, 1, 0)

        def land(self, which):
            for k, block in enumerate((3, 1, 2)):
                arrive(self.piece(block, which), self.sems, 3 * which + k)
                self.forward(block, which, 1 + 3 * which + k)

        def others(self):
            arrive(self.other(0, 1), self.sib_sems, 0)
            for which in range(2):
                for k, block in enumerate((3, 1, 2)):
                    arrive(self.other(block, which), self.sib_sems, 1 + 3 * which + k)

    right = (s, hi * 4 + (x + 1) % 4)
    left = (s, hi * 4 + (x + 3) % 4)

    def shard(block, which):
        h = hi if which == 0 else 1 - hi
        return h * 4 + (x + block) % 4

    def shard_rows(block, which):
        return pl.ds(pl.multiple_of(shard(block, which) * 192, 192), 192)

    def whole_ring(ref, ring_sems):
        return Ring(lambda block, which: ref.at[shard_rows(block, which)], ring_sems, right, left)

    def half_ring(kind, ref, ring_sems, sib_sems):
        def of(c):
            def piece(block, which):
                first = shard(block, which) * 192 + c * 96
                return ref.at[pl.ds(pl.multiple_of(first, 96), 96)]

            return piece

        return kind(of(core), ring_sems, right, left, of(1 - core), sib_sems)

    def seq_peer(d):
        return (2 * ((j + d) % 8) + core, m)

    my_rows = shard_rows(0, 0)
    own_half = pl.ds(pl.multiple_of(core * 96, 96), 96)
    widen_half = pl.ds(pl.multiple_of(core * 768, 768), 768)
    conv_half = pl.ds(pl.multiple_of(core * 48, 48), 48)
    other_widen_half = pl.ds(pl.multiple_of((1 - core) * 768, 768), 768)
    other_conv_half = pl.ds(pl.multiple_of((1 - core) * 48, 48), 48)

    local = [
        pltpu.make_async_copy(src, dst, in_sem.at[i])
        for i, (src, dst) in enumerate(
            [
                (codes_hbm, codes_i),
                (e_hbm, e_loc),
                (w_hbm, w_loc),
                (exit_hbm, exit_full.at[my_rows]),
                (narrow_hbm, narrow_loc),
                (widen_hbm, widen_all.at[hi]),
                (conv_hbm, conv_all.at[hi]),
            ]
        )
    ]
    for copy in local:
        copy.start()

    x_e = half_ring(Direct, et_full, e_sems, ef_sems)
    x_exit = half_ring(Ring, exit_full, x_sems, xf_sems)
    x_att = whole_ring(att_full, att_sems)
    x_fin = whole_ring(fin_full, fin_sems)

    barrier = pltpu.get_barrier_semaphore()
    greet = [(sib, m), (s8, m4)]
    greet += [(s, (m + d) % 8) for d in range(1, 8)]
    greet += [seq_peer(d) for d in range(1, 8)]
    for dev in greet:
        pl.semaphore_signal(barrier, inc=1, device_id=dev, device_id_type=MESH)

    rows = lax.broadcasted_iota(jnp.int32, (T, T), 0)
    cols = lax.broadcasted_iota(jnp.int32, (T, T), 1)
    order = jnp.where(rows == 4 * (cols % PATCH) + cols // PATCH, 1.0, 0.0).astype(BF)
    local[0].wait()
    codes_all[j] = codes_i[...].astype(BF)
    local[1].wait()
    et_full[my_rows, :] = dot(e_loc[...], order).astype(BF)

    local[2].wait()
    gain = g1_ref[...].astype(F32).reshape(1, D)
    wg_t[0:448, :] = (w_loc[...].astype(F32) * gain).astype(BF)
    wg_t[448:512, :] = jnp.zeros((64, D), BF)

    shard_stream = dot_nt(et_full[my_rows, :], one_hot_codes(codes_all[j])).astype(BF).astype(F32)
    squares = jnp.sum(shard_stream * shard_stream, axis=0, keepdims=True)
    sq_all[0] = squares

    pl.semaphore_wait(barrier, len(greet))

    for d in range(1, 8):
        push(sq_all.at[0], sq_all.at[d], sq_sems, d, (s, (m + d) % 8))
    x_e.start(0)
    push(x_e.piece(0, 0), x_e.piece(0, 0), w_sems, 0, (s8, m4))
    for d in (4, 1, 7, 5, 3, 2, 6):
        push(codes_all.at[j], codes_all.at[j], codes_sems, d, seq_peer(d))
    push(codes_all.at[j], codes_sib, codes_sems, 0, (sib, m))
    push(exit_hbm.at[own_half], x_exit.piece(0, 0), w_sems, 1, (s8, m4))
    push(widen_hbm.at[widen_half], widen_all.at[hi, widen_half], w_sems, 2, (s8, m4))

    local[4].wait()
    narrow_t[hi] = narrow_loc[...].T
    arrive(x_e.piece(0, 1), w_sems, 0)
    x_e.start(1)
    local[3].wait()
    x_exit.start(0)
    for d in range(1, 8):
        arrive(sq_all.at[d], sq_sems, d)
        squares = squares + sq_all[d]
    u_all[j] = squares / D + EPS
    push(u_all.at[j], u_sib, u_sems, 0, (sib, m))
    for d in range(1, 8):
        push(u_all.at[j], u_all.at[j], u_sems, d, seq_peer(d))
    x_e.land(0)
    x_e.land(1)
    x_e.others()
    arrive(x_exit.piece(0, 1), w_sems, 1)
    x_exit.start(1)

    m_t[...] = dot(wg_t[...], et_full[...]).astype(BF)

    lanes = lax.broadcasted_iota(jnp.int32, (T, 256), 1)

    def keys_values(block, at):
        hot = one_hot_codes(codes_all[block])
        raw = dot_nt(hot, m_t[128:512, :])
        spread = token_columns(u_all[block], 128)
        key = raw[:, :128]
        mean = jnp.mean(key * key, axis=1, keepdims=True)
        keys[at, :] = (key * lax.rsqrt(mean + EPS * spread)).astype(BF)
        inverse = lax.rsqrt(spread)
        value = raw[:, 128:] * jnp.concatenate([inverse, inverse], axis=1)
        vals[at, :] = jnp.where(lanes < VALUE, value, 1.0).astype(BF)

    factor = sharp_ref[0] * (LOG2E / PROBE)

    def make_queries(slot, codes, u_row):
        raw = dot_nt(one_hot_codes(codes), m_t[0:128, :])
        spread = token_columns(u_row, 128)
        mean = jnp.mean(raw * raw, axis=1, keepdims=True)
        queries[slot] = (raw * (lax.rsqrt(mean + EPS * spread) * factor)).astype(BF)

    keys_values(j, pl.ds(0, T))
    make_queries(core, codes_all[j], u_all[j])
    arrive(codes_sib, codes_sems, 0)
    arrive(u_sib, u_sems, 0)
    make_queries(1 - core, codes_sib[...], u_sib[...])
    for d in (4, 1, 7, 5, 3, 2, 6):
        block = (j + 8 - d) % 8
        arrive(codes_all.at[block], codes_sems, d)
        arrive(u_all.at[block], u_sems, d)
        keys_values(block, pl.ds(d * T, T))

    def attend(slot, half):
        asked = queries[slot, pl.ds(pl.multiple_of(half * TH, TH), TH), :]
        weights = jnp.exp2(dot_nt(asked, keys[...])).astype(BF)
        return dot(weights, vals[...])

    def exchange(slot, which):
        part_send[which] = attend(slot, 1 - core)
        push(part_send.at[which], part_recv.at[which], p_sems, which, (sib, m))

    def attended(slot, which):
        whole = attend(slot, core)
        arrive(part_recv.at[which], p_sems, which)
        whole = whole + part_recv[which]
        return (whole[:, :VALUE] / whole[:, VALUE : VALUE + 1]).astype(BF).T

    x_exit.relay(0)
    exchange(1 - hi, 1)
    att_send[...] = attended(1 - hi, 1)
    push(att_send, att_full.at[my_rows], p_sems, 2, (s, m4))
    narrow_mine = narrow_t.at[hi, widen_half]
    push(narrow_mine, narrow_mine, w_sems, 3, (s8, m4))
    push(conv_hbm.at[:, conv_half], conv_all.at[hi, :, conv_half], w_sems, 4, (s8, m4))
    exchange(hi, 0)
    x_exit.relay(1)
    att_full[my_rows, :] = attended(hi, 0)
    x_att.start(0)
    arrive(att_full.at[shard_rows(0, 1)], p_sems, 2)
    x_att.start(1)

    foreign_widen = widen_all.at[1 - hi, widen_half]
    arrive(foreign_widen, w_sems, 2)
    push(foreign_widen, foreign_widen, wf_sems, 0, (sib, m))
    x_att.relay(0)

    def group_stream(codes):
        hot = one_hot_codes(codes)

        def step(i, _):
            at = pl.ds(pl.multiple_of(i * 256, 256), 256)
            stream[:, at] = dot_nt(hot, et_full[at, :]).astype(BF)
            return 0

        lax.fori_loop(0, D // 256, step, 0)

    half_rows = pl.ds(pl.multiple_of(core * TH, TH), TH)

    @pl.when(core == hi)
    def _():
        group_stream(codes_all[j, half_rows])

    @pl.when(core != hi)
    def _():
        group_stream(codes_sib[half_rows, :])

    x_att.relay(1)
    x_exit.near()
    x_exit.opposite()
    x_exit.others()
    x_att.near()
    x_att.opposite()
    for b in range(4):
        att[:, b * 384 : (b + 1) * 384] = att_full[b * 384 : (b + 1) * 384, :].T

    def exit_step(i, total):
        at = pl.ds(pl.multiple_of(i * 256, 256), 256)
        tile = (stream[:, at].astype(F32) + dot(att[...], exit_full[:, at])).astype(BF)
        mixed[:, at] = tile
        wide = tile.astype(F32)
        return total + jnp.sum(wide * wide, axis=1, keepdims=True)

    squares = lax.fori_loop(0, D // 256, exit_step, jnp.zeros((TH, 1), F32))
    second_scale = lax.rsqrt(squares / D + EPS)
    gain = g2_ref[...].astype(F32).reshape(1, D)
    scaled = (mixed[...].astype(F32) * gain).astype(BF)
    local[5].wait()
    arrive(widen_all.at[1 - hi, other_widen_half], wf_sems, 0)
    for h in range(2):
        inner = jnp.maximum(dot(scaled, widen_all[h]) * second_scale, 0.0).astype(BF)
        inner_t[h * HIDDEN : (h + 1) * HIDDEN, :] = inner.T

    foreign_narrow = narrow_t.at[1 - hi, widen_half]
    arrive(foreign_narrow, w_sems, 3)
    push(foreign_narrow, foreign_narrow, wf_sems, 1, (sib, m))
    arrive(narrow_t.at[1 - hi, other_widen_half], wf_sems, 1)

    def partial(block, which):
        at = shard_rows(block, which)
        return dot(narrow_t[0, at, :], inner_t[:HIDDEN, :]) + dot(
            narrow_t[1, at, :], inner_t[HIDDEN:, :]
        )

    def give(index, value, dst, d, dev):
        rs_send[index] = value.astype(BF)
        push(rs_send.at[index], dst, sum_sems, d, dev)

    give(0, partial(2, 0), rs_half.at[0], 0, right)
    give(1, partial(2, 1), rs_half.at[1], 1, left)
    give(2, partial(1, 1), rs_recv.at[0, 1], 2, right)
    give(3, partial(3, 0), rs_recv.at[1, 0], 3, left)
    right_sum = partial(1, 0)
    left_sum = partial(3, 1)
    mixed_t[...] = mixed[...].T
    own = [
        partial(0, which) + mixed_t[shard_rows(0, which), :].astype(F32) for which in range(2)
    ]
    arrive(rs_half.at[0], sum_sems, 0)
    give(4, right_sum + rs_half[0].astype(F32), rs_recv.at[0, 0], 4, right)
    arrive(rs_half.at[1], sum_sems, 1)
    give(5, left_sum + rs_half[1].astype(F32), rs_recv.at[1, 1], 5, left)

    def finish(which, from_left, from_right):
        arrive(rs_recv.at[0, which], sum_sems, from_left)
        arrive(rs_recv.at[1, which], sum_sems, from_right)
        total = own[which] + rs_recv[0, which].astype(F32) + rs_recv[1, which].astype(F32)
        fin_full[shard_rows(0, which), :] = total.astype(BF)
        x_fin.start(which)

    finish(0, 4, 3)
    finish(1, 2, 5)

    next_s = (s + 16 + (1 - core) + core * (2 * hi - 1)) % 16
    prev_s = (s + 16 - core + (1 - core) * (2 * hi - 1)) % 16
    ends = [
        fin_full[pl.ds(pl.multiple_of((h * 4 + x) * 192, 192), 192), :] for h in range(2)
    ]
    halo_send[0] = jnp.concatenate([end[:, TH - 128 :].T[112:128] for end in ends], axis=1)
    halo_send[1] = jnp.concatenate([end[:, :128].T[0:16] for end in ends], axis=1)
    sides = [(next_s, (hi + core) % 2), (prev_s, (hi + 1 - core) % 2)]
    for side, (to_s, to_hi) in enumerate(sides):
        for k in range(4):
            push(
                halo_send.at[side],
                halo_recv.at[side * 4 + x],
                edge_sems,
                side * 4 + k,
                (to_s, to_hi * 4 + (x + k) % 4),
            )

    foreign_conv = conv_all.at[1 - hi, :, conv_half]
    arrive(foreign_conv, w_sems, 4)
    push(foreign_conv, foreign_conv, wf_sems, 2, (sib, m))
    x_fin.relay(0)
    x_fin.relay(1)
    local[6].wait()
    arrive(conv_all.at[1 - hi, :, other_conv_half], wf_sems, 2)
    for h in range(2):
        taps = [conv_all[h, k].astype(F32) for k in range(5)]
        folded = [
            (taps[0] + taps[1], taps[0]),
            (taps[2] + taps[3], taps[1] + taps[2]),
            (taps[4], taps[3] + taps[4]),
        ]
        for index, (even, odd) in enumerate(folded):
            conv_t[index, h * 192 : h * 192 + OUTS, :] = even.astype(BF)
            conv_t[index, h * 192 + OUTS : (h + 1) * 192, :] = odd.astype(BF)

    for side in range(2):
        for k in range(4):
            arrive(halo_recv.at[side * 4 + (x + 4 - k) % 4], edge_sems, side * 4 + k)
        row = jnp.concatenate(
            [
                halo_recv[side * 4 + chip][:, h * 192 : (h + 1) * 192]
                for h in range(2)
                for chip in range(4)
            ],
            axis=1,
        )
        added = dot_nt(row, conv_t[2 * side]).T
        column = added[:, 15:16] if side == 0 else added[:, 0:1]
        edges[side] = jnp.broadcast_to(column, (4 * OUTS, 128))

    x_fin.near()
    x_fin.opposite()

    place = 4 * j + 2 * hi + core
    rows = lax.broadcasted_iota(jnp.int32, (256, 256), 0)
    cols = lax.broadcasted_iota(jnp.int32, (256, 256), 1)
    weave = jnp.where(cols == 2 * (rows % 128) + rows // 128, 1.0, 0.0).astype(BF)

    def taps_of(which):
        h = hi if which == 0 else 1 - hi
        at = pl.ds(pl.multiple_of(h * 192, 192), 192)
        return at, [dot(conv_t[k, at, :], fin_full[...]) for k in range(3)]

    def outputs(at, products):
        before, here, after = products
        left_edge = jnp.where(place > 0, edges[0, at, :][:, 0:1], 0.0)
        right_edge = jnp.where(place < 31, edges[1, at, :][:, 0:1], 0.0)
        before = jnp.concatenate([left_edge, before[:, : TH - 1]], axis=1)
        after = jnp.concatenate([after[:, 1:], right_edge], axis=1)
        result = (before + here + after).astype(BF)
        woven = []
        for b in range(2):
            span = slice(b * 128, (b + 1) * 128)
            both = jnp.concatenate([result[:OUTS, span], result[OUTS:, span]], axis=1)
            woven.append(dot(both, weave).astype(BF))
        return jnp.concatenate(woven, axis=1)

    out_send[1] = outputs(*taps_of(1))
    push(out_send.at[1], out_recv.at[core], out_sems, 4 + core, (2 * j + hi, m4))
    mine = outputs(*taps_of(0))
    out_send[0] = mine
    to_sibling = send(out_send.at[0], out_recv.at[core], out_sems, 2 + core, (sib, m))

    @pl.when(core == hi)
    def _():
        out_ref[:, pl.ds(pl.multiple_of(core * T, T), T)] = mine
        arrive(out_recv.at[1 - core], out_sems, 3 - core)
        out_ref[:, pl.ds(pl.multiple_of((1 - core) * T, T), T)] = out_recv[1 - core]

    @pl.when(core != hi)
    def _():
        to_sibling.start()
        arrive(out_recv.at[0], out_sems, 4)
        arrive(out_recv.at[1], out_sems, 5)
        out_ref[:, :T] = out_recv[0]
        out_ref[:, T:] = out_recv[1]
        to_sibling.wait_send()

    for copy in pending:
        copy.wait_send()


def per_device(codes, e, g1, w, sharp, exit_map, g2, widen, narrow, conv):
    any_space = pl.BlockSpec(memory_space=pl.ANY)
    vmem = pl.BlockSpec(memory_space=pltpu.VMEM)
    smem = pl.BlockSpec(memory_space=pltpu.SMEM)
    dma = pltpu.SemaphoreType.DMA((8,))
    return pl.pallas_call(
        kernel,
        out_shape=jax.ShapeDtypeStruct((OUTS, 2 * T), BF),
        in_specs=[
            any_space,
            any_space,
            vmem,
            any_space,
            smem,
            any_space,
            vmem,
            any_space,
            any_space,
            any_space,
        ],
        out_specs=vmem,
        scratch_shapes=[
            pltpu.VMEM((T, PATCH), jnp.int32),
            pltpu.VMEM((8, T, PATCH), BF),
            pltpu.VMEM((T, PATCH), BF),
            pltpu.VMEM((192, T), BF),
            pltpu.VMEM((D, T), BF),
            pltpu.VMEM((448, D), BF),
            pltpu.VMEM((T, D), BF),
            pltpu.VMEM((T, T), BF),
            pltpu.VMEM((D, D), BF),
            pltpu.VMEM((TH, D), BF),
            pltpu.VMEM((8, 1, T), F32),
            pltpu.VMEM((8, 1, T), F32),
            pltpu.VMEM((1, T), F32),
            pltpu.VMEM((8 * T, PROBE), BF),
            pltpu.VMEM((8 * T, 256), BF),
            pltpu.VMEM((2, T, PROBE), BF),
            pltpu.VMEM((2, TH, 256), F32),
            pltpu.VMEM((2, TH, 256), F32),
            pltpu.VMEM((192, TH), BF),
            pltpu.VMEM((D, TH), BF),
            pltpu.VMEM((TH, D), BF),
            pltpu.VMEM((TH, D), BF),
            pltpu.VMEM((D, TH), BF),
            pltpu.VMEM((2, D, HIDDEN), BF),
            pltpu.VMEM((HIDDEN, D), BF),
            pltpu.VMEM((2, D, HIDDEN), BF),
            pltpu.VMEM((2 * HIDDEN, TH), BF),
            pltpu.VMEM((6, 192, TH), BF),
            pltpu.VMEM((2, 192, TH), BF),
            pltpu.VMEM((2, 2, 192, TH), BF),
            pltpu.VMEM((D, TH), BF),
            pltpu.VMEM((2, 5, OUTS, D), BF),
            pltpu.VMEM((3, 4 * OUTS, D), BF),
            pltpu.VMEM((2, 16, 2 * 192), BF),
            pltpu.VMEM((8, 16, 2 * 192), BF),
            pltpu.VMEM((2, 4 * OUTS, 128), F32),
            pltpu.VMEM((2, OUTS, T), BF),
            pltpu.VMEM((2, OUTS, T), BF),
        ]
        + [dma] * 31,
        compiler_params=pltpu.CompilerParams(
            collective_id=0, has_side_effects=True, vmem_limit_bytes=60 * 1024 * 1024
        ),
        cost_estimate=pl.CostEstimate(
            flops=8_000_000_000, bytes_accessed=8_000_000, transcendentals=4_000_000
        ),
        name="genomic_forward",
    )(
        codes.reshape(T, PATCH),
        e.T,
        g1,
        w.T,
        sharp,
        exit_map,
        g2,
        widen,
        narrow,
        conv.transpose(0, 2, 1),
    )


def solution(mesh):
    in_specs = (
        P("seq"),
        P(None, "mp"),
        P(),
        P(None, "mp"),
        P("mp"),
        P("mp", None),
        P(),
        P(None, "mp"),
        P("mp", None),
        P(None, None, "mp"),
    )
    return jax.shard_map(
        per_device, mesh=mesh, in_specs=in_specs, out_specs=P("mp", "seq"), check_vma=False
    )
```

```python
import jax
import jax.numpy as jnp
from jax import lax
from jax.experimental import pallas as pl
from jax.experimental.pallas import tpu as pltpu
from jax.sharding import PartitionSpec as P

MESH = pl.DeviceIdType.MESH
BF = jnp.bfloat16
F32 = jnp.float32

D = 1536
T = 512
TH = 256
PROBE = 128
VALUE = 192
HIDDEN = 384
OUTS = 96
PATCH = 128
EPS = 1e-06
LOG2E = 1.4426950408889634


def dot(a, b):
    return jnp.dot(a, b, preferred_element_type=F32)


def dot_nt(a, b):
    return lax.dot_general(a, b, (((1,), (1,)), ((), ())), preferred_element_type=F32)


def dot_tn(a, b):
    return lax.dot_general(a, b, (((0,), (0,)), ((), ())), preferred_element_type=F32)


def one_hot_codes(codes):
    wide = codes.astype(F32)
    parts = [jnp.where(wide == float(b), 1.0, 0.0).astype(BF) for b in range(4)]
    return jnp.concatenate(parts, axis=1)


def token_columns(row, width):
    high = row.astype(BF)
    low = (row - high.astype(F32)).astype(BF)
    both = jnp.concatenate(
        [jnp.broadcast_to(high, (16, T)), jnp.broadcast_to(low, (16, T))], axis=0
    )
    return dot_tn(both, jnp.full((32, width), 1.0 / 16.0, BF))


def kernel(
    codes_hbm,
    e_hbm,
    g1_ref,
    w_hbm,
    sharp_ref,
    exit_hbm,
    g2_ref,
    widen_hbm,
    narrow_hbm,
    conv_hbm,
    out_ref,
    codes_i,
    codes_all,
    codes_sib,
    e_loc,
    et_full,
    w_loc,
    wg_t,
    m_t,
    exit_full,
    stream,
    sq_all,
    u_all,
    u_sib,
    keys,
    vals,
    queries,
    part_send,
    part_recv,
    att_send,
    att_full,
    att,
    mixed,
    mixed_t,
    widen_all,
    narrow_loc,
    narrow_t,
    inner_t,
    rs_send,
    rs_half,
    rs_recv,
    fin_full,
    conv_all,
    conv_t,
    halo_send,
    halo_recv,
    edges,
    out_send,
    out_recv,
    in_sem,
    *sems,
):
    pairs = [sems[2 * i : 2 * i + 2] for i in range(15)]
    codes_sems, w_sems, wf_sems, e_sems, ef_sems, x_sems = pairs[:6]
    xf_sems, u_sems, p_sems, att_sems, sum_sems, fin_sems, edge_sems, sq_sems = pairs[6:14]
    out_sems = pairs[14]

    s = lax.axis_index("seq")
    m = lax.axis_index("mp")
    core = s % 2
    j = s // 2
    z = j % 4
    y_lo = j // 4
    x = m % 4
    hi = m // 4
    sib = s + 1 - 2 * core
    m4 = (m + 4) % 8
    s8 = (s + 8) % 16

    def send(src, dst, sems, d, dev):
        return pltpu.make_async_remote_copy(
            src_ref=src,
            dst_ref=dst,
            send_sem=sems[0].at[d],
            recv_sem=sems[1].at[d],
            device_id=dev,
            device_id_type=MESH,
        )

    pending = []

    def push(src, dst, sems, d, dev):
        copy = send(src, dst, sems, d, dev)
        copy.start()
        pending.append(copy)

    def arrive(dst, sems, d):
        send(dst, dst, sems, d, (sib, m)).wait_recv()

    class Ring:
        def __init__(self, piece, sems, right, left, other=None, sib_sems=None):
            self.piece, self.sems, self.right, self.left = piece, sems, right, left
            self.other, self.sib_sems = other, sib_sems

        def go(self, block, which, d, dev):
            push(self.piece(block, which), self.piece(block, which), self.sems, d, dev)

        def forward(self, block, which, d):
            if self.sib_sems is not None:
                piece = self.piece(block, which)
                push(piece, piece, self.sib_sems, d, (sib, m))

        def start(self, which):
            if which == 0:
                self.go(0, 0, 0, self.right)
                self.go(0, 0, 3, self.left)
            else:
                self.go(0, 1, 1, self.left)
                self.go(0, 1, 2, self.right)
                self.forward(0, 1, 0)

        def relay(self, which):
            if which == 0:
                arrive(self.piece(3, 0), self.sems, 0)
                self.go(3, 0, 4, self.right)
                self.forward(3, 0, 1)
            else:
                arrive(self.piece(1, 1), self.sems, 1)
                self.go(1, 1, 5, self.left)
                self.forward(1, 1, 2)

        def near(self):
            arrive(self.piece(1, 0), self.sems, 3)
            self.forward(1, 0, 3)
            arrive(self.piece(3, 1), self.sems, 2)
            self.forward(3, 1, 4)

        def opposite(self):
            arrive(self.piece(2, 0), self.sems, 4)
            self.forward(2, 0, 5)
            arrive(self.piece(2, 1), self.sems, 5)
            self.forward(2, 1, 6)

        def others(self):
            order = [(0, 1), (3, 0), (1, 1), (1, 0), (3, 1), (2, 0), (2, 1)]
            for d, (block, which) in enumerate(order):
                arrive(self.other(block, which), self.sib_sems, d)

    class Direct(Ring):
        def start(self, which):
            across = (s, hi * 4 + (x + 2) % 4)
            for k, dev in enumerate((self.right, self.left, across)):
                self.go(0, which, 3 * which + k, dev)
            if which == 1:
                self.forward(0, 1, 0)

        def land(self, which):
            for k, block in enumerate((3, 1, 2)):
                arrive(self.piece(block, which), self.sems, 3 * which + k)
                self.forward(block, which, 1 + 3 * which + k)

        def others(self):
            arrive(self.other(0, 1), self.sib_sems, 0)
            for which in range(2):
                for k, block in enumerate((3, 1, 2)):
                    arrive(self.other(block, which), self.sib_sems, 1 + 3 * which + k)

    right = (s, hi * 4 + (x + 1) % 4)
    left = (s, hi * 4 + (x + 3) % 4)

    def shard(block, which):
        h = hi if which == 0 else 1 - hi
        return h * 4 + (x + block) % 4

    def shard_rows(block, which):
        return pl.ds(pl.multiple_of(shard(block, which) * 192, 192), 192)

    def whole_ring(ref, ring_sems):
        return Ring(lambda block, which: ref.at[shard_rows(block, which)], ring_sems, right, left)

    def half_ring(kind, ref, ring_sems, sib_sems):
        def of(c):
            def piece(block, which):
                first = shard(block, which) * 192 + c * 96
                return ref.at[pl.ds(pl.multiple_of(first, 96), 96)]

            return piece

        return kind(of(core), ring_sems, right, left, of(1 - core), sib_sems)

    def seq_peer(d):
        return (2 * ((j + d) % 8) + core, m)

    my_rows = shard_rows(0, 0)
    own_half = pl.ds(pl.multiple_of(core * 96, 96), 96)
    widen_half = pl.ds(pl.multiple_of(core * 768, 768), 768)
    conv_half = pl.ds(pl.multiple_of(core * 48, 48), 48)
    other_widen_half = pl.ds(pl.multiple_of((1 - core) * 768, 768), 768)
    other_conv_half = pl.ds(pl.multiple_of((1 - core) * 48, 48), 48)

    local = [
        pltpu.make_async_copy(src, dst, in_sem.at[i])
        for i, (src, dst) in enumerate(
            [
                (codes_hbm, codes_i),
                (e_hbm, e_loc),
                (w_hbm, w_loc),
                (exit_hbm, exit_full.at[my_rows]),
                (narrow_hbm, narrow_loc),
                (widen_hbm, widen_all.at[hi]),
                (conv_hbm, conv_all.at[hi]),
            ]
        )
    ]
    for copy in local:
        copy.start()

    x_e = half_ring(Direct, et_full, e_sems, ef_sems)
    x_exit = half_ring(Ring, exit_full, x_sems, xf_sems)
    x_att = whole_ring(att_full, att_sems)
    x_fin = whole_ring(fin_full, fin_sems)

    barrier = pltpu.get_barrier_semaphore()
    greet = [(sib, m), (s8, m4)]
    greet += [(s, (m + d) % 8) for d in range(1, 8)]
    greet += [seq_peer(d) for d in range(1, 8)]
    for dev in greet:
        pl.semaphore_signal(barrier, inc=1, device_id=dev, device_id_type=MESH)

    rows = lax.broadcasted_iota(jnp.int32, (T, T), 0)
    cols = lax.broadcasted_iota(jnp.int32, (T, T), 1)
    order = jnp.where(rows == 4 * (cols % PATCH) + cols // PATCH, 1.0, 0.0).astype(BF)
    local[0].wait()
    codes_all[j] = codes_i[...].astype(BF)
    local[1].wait()
    et_full[my_rows, :] = dot(e_loc[...], order).astype(BF)

    local[2].wait()
    gain = g1_ref[...].astype(F32).reshape(1, D)
    wg_t[0:448, :] = (w_loc[...].astype(F32) * gain).astype(BF)
    wg_t[448:512, :] = jnp.zeros((64, D), BF)

    shard_stream = dot_nt(et_full[my_rows, :], one_hot_codes(codes_all[j])).astype(BF).astype(F32)
    squares = jnp.sum(shard_stream * shard_stream, axis=0, keepdims=True)
    sq_all[0] = squares

    pl.semaphore_wait(barrier, len(greet))

    for d in range(1, 8):
        push(sq_all.at[0], sq_all.at[d], sq_sems, d, (s, (m + d) % 8))
    x_e.start(0)
    push(x_e.piece(0, 0), x_e.piece(0, 0), w_sems, 0, (s8, m4))
    for d in (4, 1, 7, 5, 3, 2, 6):
        push(codes_all.at[j], codes_all.at[j], codes_sems, d, seq_peer(d))
    push(codes_all.at[j], codes_sib, codes_sems, 0, (sib, m))
    push(exit_hbm.at[own_half], x_exit.piece(0, 0), w_sems, 1, (s8, m4))
    push(widen_hbm.at[widen_half], widen_all.at[hi, widen_half], w_sems, 2, (s8, m4))

    local[4].wait()
    narrow_t[hi] = narrow_loc[...].T
    arrive(x_e.piece(0, 1), w_sems, 0)
    x_e.start(1)
    local[3].wait()
    x_exit.start(0)
    for d in range(1, 8):
        arrive(sq_all.at[d], sq_sems, d)
        squares = squares + sq_all[d]
    u_all[j] = squares / D + EPS
    push(u_all.at[j], u_sib, u_sems, 0, (sib, m))
    for d in range(1, 8):
        push(u_all.at[j], u_all.at[j], u_sems, d, seq_peer(d))
    x_e.land(0)
    x_e.land(1)
    x_e.others()
    arrive(x_exit.piece(0, 1), w_sems, 1)
    x_exit.start(1)

    m_t[...] = dot(wg_t[...], et_full[...]).astype(BF)

    lanes = lax.broadcasted_iota(jnp.int32, (T, 256), 1)

    def keys_values(block, at):
        hot = one_hot_codes(codes_all[block])
        raw = dot_nt(hot, m_t[128:512, :])
        spread = token_columns(u_all[block], 128)
        key = raw[:, :128]
        mean = jnp.mean(key * key, axis=1, keepdims=True)
        keys[at, :] = (key * lax.rsqrt(mean + EPS * spread)).astype(BF)
        inverse = lax.rsqrt(spread)
        value = raw[:, 128:] * jnp.concatenate([inverse, inverse], axis=1)
        vals[at, :] = jnp.where(lanes < VALUE, value, 1.0).astype(BF)

    factor = sharp_ref[0] * (LOG2E / PROBE)

    def make_queries(slot, codes, u_row):
        raw = dot_nt(one_hot_codes(codes), m_t[0:128, :])
        spread = token_columns(u_row, 128)
        mean = jnp.mean(raw * raw, axis=1, keepdims=True)
        queries[slot] = (raw * (lax.rsqrt(mean + EPS * spread) * factor)).astype(BF)

    keys_values(j, pl.ds(0, T))
    make_queries(core, codes_all[j], u_all[j])
    arrive(codes_sib, codes_sems, 0)
    arrive(u_sib, u_sems, 0)
    make_queries(1 - core, codes_sib[...], u_sib[...])
    for d in (4, 1, 7, 5, 3, 2, 6):
        block = (j + 8 - d) % 8
        arrive(codes_all.at[block], codes_sems, d)
        arrive(u_all.at[block], u_sems, d)
        keys_values(block, pl.ds(d * T, T))

    def attend(slot, half):
        asked = queries[slot, pl.ds(pl.multiple_of(half * TH, TH), TH), :]
        weights = jnp.exp2(dot_nt(asked, keys[...])).astype(BF)
        return dot(weights, vals[...])

    def exchange(slot, which):
        part_send[which] = attend(slot, 1 - core)
        push(part_send.at[which], part_recv.at[which], p_sems, which, (sib, m))

    def attended(slot, which):
        whole = attend(slot, core)
        arrive(part_recv.at[which], p_sems, which)
        whole = whole + part_recv[which]
        return (whole[:, :VALUE] / whole[:, VALUE : VALUE + 1]).astype(BF).T

    x_exit.relay(0)
    exchange(1 - hi, 1)
    att_send[...] = attended(1 - hi, 1)
    push(att_send, att_full.at[my_rows], p_sems, 2, (s, m4))
    narrow_mine = narrow_t.at[hi, widen_half]
    push(narrow_mine, narrow_mine, w_sems, 3, (s8, m4))
    push(conv_hbm.at[:, conv_half], conv_all.at[hi, :, conv_half], w_sems, 4, (s8, m4))
    exchange(hi, 0)
    x_exit.relay(1)
    own_attended = attended(hi, 0)
    arrive(att_full.at[shard_rows(0, 1)], p_sems, 2)
    x_att.start(1)
    att_full[my_rows, :] = own_attended
    x_att.start(0)

    foreign_widen = widen_all.at[1 - hi, widen_half]
    arrive(foreign_widen, w_sems, 2)
    push(foreign_widen, foreign_widen, wf_sems, 0, (sib, m))
    x_att.relay(0)

    def group_stream(codes):
        hot = one_hot_codes(codes)

        def step(i, _):
            at = pl.ds(pl.multiple_of(i * 256, 256), 256)
            stream[:, at] = dot_nt(hot, et_full[at, :]).astype(BF)
            return 0

        lax.fori_loop(0, D // 256, step, 0)

    half_rows = pl.ds(pl.multiple_of(core * TH, TH), TH)

    @pl.when(core == hi)
    def _():
        group_stream(codes_all[j, half_rows])

    @pl.when(core != hi)
    def _():
        group_stream(codes_sib[half_rows, :])

    x_att.relay(1)
    x_exit.near()
    x_exit.opposite()
    x_exit.others()
    x_att.near()
    x_att.opposite()
    for b in range(4):
        att[:, b * 384 : (b + 1) * 384] = att_full[b * 384 : (b + 1) * 384, :].T

    def exit_step(i, total):
        at = pl.ds(pl.multiple_of(i * 256, 256), 256)
        tile = (stream[:, at].astype(F32) + dot(att[...], exit_full[:, at])).astype(BF)
        mixed[:, at] = tile
        wide = tile.astype(F32)
        return total + jnp.sum(wide * wide, axis=1, keepdims=True)

    squares = lax.fori_loop(0, D // 256, exit_step, jnp.zeros((TH, 1), F32))
    second_scale = lax.rsqrt(squares / D + EPS)
    gain = g2_ref[...].astype(F32).reshape(1, D)
    scaled = (mixed[...].astype(F32) * gain).astype(BF)
    local[5].wait()
    arrive(widen_all.at[1 - hi, other_widen_half], wf_sems, 0)
    for h in range(2):
        inner = jnp.maximum(dot(scaled, widen_all[h]) * second_scale, 0.0).astype(BF)
        inner_t[h * HIDDEN : (h + 1) * HIDDEN, :] = inner.T

    foreign_narrow = narrow_t.at[1 - hi, widen_half]
    arrive(foreign_narrow, w_sems, 3)
    push(foreign_narrow, foreign_narrow, wf_sems, 1, (sib, m))
    arrive(narrow_t.at[1 - hi, other_widen_half], wf_sems, 1)

    def partial(block, which):
        at = shard_rows(block, which)
        return dot(narrow_t[0, at, :], inner_t[:HIDDEN, :]) + dot(
            narrow_t[1, at, :], inner_t[HIDDEN:, :]
        )

    def give(index, value, dst, d, dev):
        rs_send[index] = value.astype(BF)
        push(rs_send.at[index], dst, sum_sems, d, dev)

    give(0, partial(2, 0), rs_half.at[0], 0, right)
    give(1, partial(2, 1), rs_half.at[1], 1, left)
    give(2, partial(1, 1), rs_recv.at[0, 1], 2, right)
    give(3, partial(3, 0), rs_recv.at[1, 0], 3, left)
    right_sum = partial(1, 0)
    left_sum = partial(3, 1)
    mixed_t[...] = mixed[...].T
    own = [
        partial(0, which) + mixed_t[shard_rows(0, which), :].astype(F32) for which in range(2)
    ]
    arrive(rs_half.at[0], sum_sems, 0)
    give(4, right_sum + rs_half[0].astype(F32), rs_recv.at[0, 0], 4, right)
    arrive(rs_half.at[1], sum_sems, 1)
    give(5, left_sum + rs_half[1].astype(F32), rs_recv.at[1, 1], 5, left)

    def finish(which, from_left, from_right):
        arrive(rs_recv.at[0, which], sum_sems, from_left)
        arrive(rs_recv.at[1, which], sum_sems, from_right)
        total = own[which] + rs_recv[0, which].astype(F32) + rs_recv[1, which].astype(F32)
        fin_full[shard_rows(0, which), :] = total.astype(BF)
        x_fin.start(which)

    finish(0, 4, 3)
    finish(1, 2, 5)

    next_s = (s + 16 + (1 - core) + core * (2 * hi - 1)) % 16
    prev_s = (s + 16 - core + (1 - core) * (2 * hi - 1)) % 16
    ends = [
        fin_full[pl.ds(pl.multiple_of((h * 4 + x) * 192, 192), 192), :] for h in range(2)
    ]
    halo_send[0] = jnp.concatenate([end[:, TH - 128 :].T[112:128] for end in ends], axis=1)
    halo_send[1] = jnp.concatenate([end[:, :128].T[0:16] for end in ends], axis=1)
    sides = [(next_s, (hi + core) % 2), (prev_s, (hi + 1 - core) % 2)]
    for side, (to_s, to_hi) in enumerate(sides):
        for k in range(4):
            push(
                halo_send.at[side],
                halo_recv.at[side * 4 + x],
                edge_sems,
                side * 4 + k,
                (to_s, to_hi * 4 + (x + k) % 4),
            )

    foreign_conv = conv_all.at[1 - hi, :, conv_half]
    arrive(foreign_conv, w_sems, 4)
    push(foreign_conv, foreign_conv, wf_sems, 2, (sib, m))
    x_fin.relay(0)
    x_fin.relay(1)
    local[6].wait()
    arrive(conv_all.at[1 - hi, :, other_conv_half], wf_sems, 2)
    for h in range(2):
        taps = [conv_all[h, k].astype(F32) for k in range(5)]
        folded = [
            (taps[0] + taps[1], taps[0]),
            (taps[2] + taps[3], taps[1] + taps[2]),
            (taps[4], taps[3] + taps[4]),
        ]
        for index, (even, odd) in enumerate(folded):
            conv_t[index, h * 192 : h * 192 + OUTS, :] = even.astype(BF)
            conv_t[index, h * 192 + OUTS : (h + 1) * 192, :] = odd.astype(BF)

    for side in range(2):
        for k in range(4):
            arrive(halo_recv.at[side * 4 + (x + 4 - k) % 4], edge_sems, side * 4 + k)
        row = jnp.concatenate(
            [
                halo_recv[side * 4 + chip][:, h * 192 : (h + 1) * 192]
                for h in range(2)
                for chip in range(4)
            ],
            axis=1,
        )
        added = dot_nt(row, conv_t[2 * side]).T
        column = added[:, 15:16] if side == 0 else added[:, 0:1]
        edges[side] = jnp.broadcast_to(column, (4 * OUTS, 128))

    x_fin.near()
    x_fin.opposite()

    place = 4 * j + 2 * hi + core
    rows = lax.broadcasted_iota(jnp.int32, (256, 256), 0)
    cols = lax.broadcasted_iota(jnp.int32, (256, 256), 1)
    weave = jnp.where(cols == 2 * (rows % 128) + rows // 128, 1.0, 0.0).astype(BF)

    def taps_of(which):
        h = hi if which == 0 else 1 - hi
        at = pl.ds(pl.multiple_of(h * 192, 192), 192)
        return at, [dot(conv_t[k, at, :], fin_full[...]) for k in range(3)]

    def outputs(at, products):
        before, here, after = products
        left_edge = jnp.where(place > 0, edges[0, at, :][:, 0:1], 0.0)
        right_edge = jnp.where(place < 31, edges[1, at, :][:, 0:1], 0.0)
        before = jnp.concatenate([left_edge, before[:, : TH - 1]], axis=1)
        after = jnp.concatenate([after[:, 1:], right_edge], axis=1)
        result = (before + here + after).astype(BF)
        woven = []
        for b in range(2):
            span = slice(b * 128, (b + 1) * 128)
            both = jnp.concatenate([result[:OUTS, span], result[OUTS:, span]], axis=1)
            woven.append(dot(both, weave).astype(BF))
        return jnp.concatenate(woven, axis=1)

    out_send[1] = outputs(*taps_of(1))
    push(out_send.at[1], out_recv.at[core], out_sems, 4 + core, (2 * j + hi, m4))
    mine = outputs(*taps_of(0))
    out_send[0] = mine
    to_sibling = send(out_send.at[0], out_recv.at[core], out_sems, 2 + core, (sib, m))

    @pl.when(core == hi)
    def _():
        out_ref[:, pl.ds(pl.multiple_of(core * T, T), T)] = mine
        arrive(out_recv.at[1 - core], out_sems, 3 - core)
        out_ref[:, pl.ds(pl.multiple_of((1 - core) * T, T), T)] = out_recv[1 - core]

    @pl.when(core != hi)
    def _():
        to_sibling.start()
        arrive(out_recv.at[0], out_sems, 4)
        arrive(out_recv.at[1], out_sems, 5)
        out_ref[:, :T] = out_recv[0]
        out_ref[:, T:] = out_recv[1]
        to_sibling.wait_send()

    for copy in pending:
        copy.wait_send()


def per_device(codes, e, g1, w, sharp, exit_map, g2, widen, narrow, conv):
    any_space = pl.BlockSpec(memory_space=pl.ANY)
    vmem = pl.BlockSpec(memory_space=pltpu.VMEM)
    smem = pl.BlockSpec(memory_space=pltpu.SMEM)
    dma = pltpu.SemaphoreType.DMA((8,))
    return pl.pallas_call(
        kernel,
        out_shape=jax.ShapeDtypeStruct((OUTS, 2 * T), BF),
        in_specs=[
            any_space,
            any_space,
            vmem,
            any_space,
            smem,
            any_space,
            vmem,
            any_space,
            any_space,
            any_space,
        ],
        out_specs=vmem,
        scratch_shapes=[
            pltpu.VMEM((T, PATCH), jnp.int32),
            pltpu.VMEM((8, T, PATCH), BF),
            pltpu.VMEM((T, PATCH), BF),
            pltpu.VMEM((192, T), BF),
            pltpu.VMEM((D, T), BF),
            pltpu.VMEM((448, D), BF),
            pltpu.VMEM((T, D), BF),
            pltpu.VMEM((T, T), BF),
            pltpu.VMEM((D, D), BF),
            pltpu.VMEM((TH, D), BF),
            pltpu.VMEM((8, 1, T), F32),
            pltpu.VMEM((8, 1, T), F32),
            pltpu.VMEM((1, T), F32),
            pltpu.VMEM((8 * T, PROBE), BF),
            pltpu.VMEM((8 * T, 256), BF),
            pltpu.VMEM((2, T, PROBE), BF),
            pltpu.VMEM((2, TH, 256), F32),
            pltpu.VMEM((2, TH, 256), F32),
            pltpu.VMEM((192, TH), BF),
            pltpu.VMEM((D, TH), BF),
            pltpu.VMEM((TH, D), BF),
            pltpu.VMEM((TH, D), BF),
            pltpu.VMEM((D, TH), BF),
            pltpu.VMEM((2, D, HIDDEN), BF),
            pltpu.VMEM((HIDDEN, D), BF),
            pltpu.VMEM((2, D, HIDDEN), BF),
            pltpu.VMEM((2 * HIDDEN, TH), BF),
            pltpu.VMEM((6, 192, TH), BF),
            pltpu.VMEM((2, 192, TH), BF),
            pltpu.VMEM((2, 2, 192, TH), BF),
            pltpu.VMEM((D, TH), BF),
            pltpu.VMEM((2, 5, OUTS, D), BF),
            pltpu.VMEM((3, 4 * OUTS, D), BF),
            pltpu.VMEM((2, 16, 2 * 192), BF),
            pltpu.VMEM((8, 16, 2 * 192), BF),
            pltpu.VMEM((2, 4 * OUTS, 128), F32),
            pltpu.VMEM((2, OUTS, T), BF),
            pltpu.VMEM((2, OUTS, T), BF),
        ]
        + [dma] * 31,
        compiler_params=pltpu.CompilerParams(
            collective_id=0, has_side_effects=True, vmem_limit_bytes=60 * 1024 * 1024
        ),
        cost_estimate=pl.CostEstimate(
            flops=8_000_000_000, bytes_accessed=8_000_000, transcendentals=4_000_000
        ),
        name="genomic_forward",
    )(
        codes.reshape(T, PATCH),
        e.T,
        g1,
        w.T,
        sharp,
        exit_map,
        g2,
        widen,
        narrow,
        conv.transpose(0, 2, 1),
    )


def solution(mesh):
    in_specs = (
        P("seq"),
        P(None, "mp"),
        P(),
        P(None, "mp"),
        P("mp"),
        P("mp", None),
        P(),
        P(None, "mp"),
        P("mp", None),
        P(None, None, "mp"),
    )
    return jax.shard_map(
        per_device, mesh=mesh, in_specs=in_specs, out_specs=P("mp", "seq"), check_vma=False
    )
```

```python
import jax
import jax.numpy as jnp
from jax import lax
from jax.experimental import pallas as pl
from jax.experimental.pallas import tpu as pltpu
from jax.sharding import PartitionSpec as P

MESH = pl.DeviceIdType.MESH
BF = jnp.bfloat16
F32 = jnp.float32

D = 1536
T = 512
TH = 256
PROBE = 128
VALUE = 192
HIDDEN = 384
OUTS = 96
PATCH = 128
EPS = 1e-06
LOG2E = 1.4426950408889634


def dot(a, b):
    return jnp.dot(a, b, preferred_element_type=F32)


def dot_nt(a, b):
    return lax.dot_general(a, b, (((1,), (1,)), ((), ())), preferred_element_type=F32)


def dot_tn(a, b):
    return lax.dot_general(a, b, (((0,), (0,)), ((), ())), preferred_element_type=F32)


def one_hot_codes(codes):
    wide = codes.astype(F32)
    parts = [jnp.where(wide == float(b), 1.0, 0.0).astype(BF) for b in range(4)]
    return jnp.concatenate(parts, axis=1)


def token_columns(row, width):
    high = row.astype(BF)
    low = (row - high.astype(F32)).astype(BF)
    both = jnp.concatenate(
        [jnp.broadcast_to(high, (16, T)), jnp.broadcast_to(low, (16, T))], axis=0
    )
    return dot_tn(both, jnp.full((32, width), 1.0 / 16.0, BF))


def kernel(
    codes_hbm,
    e_hbm,
    g1_ref,
    w_hbm,
    sharp_ref,
    exit_hbm,
    g2_ref,
    widen_hbm,
    narrow_hbm,
    conv_hbm,
    out_ref,
    codes_i,
    codes_all,
    codes_sib,
    e_loc,
    et_full,
    w_loc,
    wg_t,
    m_t,
    exit_full,
    stream,
    sq_all,
    u_all,
    u_sib,
    keys,
    vals,
    queries,
    part_send,
    part_recv,
    att_send,
    att_full,
    att,
    mixed,
    mixed_t,
    widen_all,
    narrow_loc,
    narrow_t,
    inner_t,
    rs_send,
    rs_half,
    rs_recv,
    fin_full,
    conv_all,
    conv_t,
    halo_send,
    halo_recv,
    edges,
    out_send,
    out_recv,
    in_sem,
    *sems,
):
    pairs = [sems[2 * i : 2 * i + 2] for i in range(15)]
    codes_sems, w_sems, wf_sems, e_sems, ef_sems, x_sems = pairs[:6]
    xf_sems, u_sems, p_sems, att_sems, sum_sems, fin_sems, edge_sems, sq_sems = pairs[6:14]
    out_sems = pairs[14]

    s = lax.axis_index("seq")
    m = lax.axis_index("mp")
    core = s % 2
    j = s // 2
    z = j % 4
    y_lo = j // 4
    x = m % 4
    hi = m // 4
    sib = s + 1 - 2 * core
    m4 = (m + 4) % 8
    s8 = (s + 8) % 16

    def send(src, dst, sems, d, dev):
        return pltpu.make_async_remote_copy(
            src_ref=src,
            dst_ref=dst,
            send_sem=sems[0].at[d],
            recv_sem=sems[1].at[d],
            device_id=dev,
            device_id_type=MESH,
        )

    pending = []

    def push(src, dst, sems, d, dev):
        copy = send(src, dst, sems, d, dev)
        copy.start()
        pending.append(copy)

    def arrive(dst, sems, d):
        send(dst, dst, sems, d, (sib, m)).wait_recv()

    class Ring:
        def __init__(self, piece, sems, right, left, other=None, sib_sems=None):
            self.piece, self.sems, self.right, self.left = piece, sems, right, left
            self.other, self.sib_sems = other, sib_sems

        def go(self, block, which, d, dev):
            push(self.piece(block, which), self.piece(block, which), self.sems, d, dev)

        def forward(self, block, which, d):
            if self.sib_sems is not None:
                piece = self.piece(block, which)
                push(piece, piece, self.sib_sems, d, (sib, m))

        def start(self, which):
            if which == 0:
                self.go(0, 0, 0, self.right)
                self.go(0, 0, 3, self.left)
            else:
                self.go(0, 1, 1, self.left)
                self.go(0, 1, 2, self.right)
                self.forward(0, 1, 0)

        def relay(self, which):
            if which == 0:
                arrive(self.piece(3, 0), self.sems, 0)
                self.go(3, 0, 4, self.right)
                self.forward(3, 0, 1)
            else:
                arrive(self.piece(1, 1), self.sems, 1)
                self.go(1, 1, 5, self.left)
                self.forward(1, 1, 2)

        def near(self):
            arrive(self.piece(1, 0), self.sems, 3)
            self.forward(1, 0, 3)
            arrive(self.piece(3, 1), self.sems, 2)
            self.forward(3, 1, 4)

        def opposite(self):
            arrive(self.piece(2, 0), self.sems, 4)
            self.forward(2, 0, 5)
            arrive(self.piece(2, 1), self.sems, 5)
            self.forward(2, 1, 6)

        def others(self):
            order = [(0, 1), (3, 0), (1, 1), (1, 0), (3, 1), (2, 0), (2, 1)]
            for d, (block, which) in enumerate(order):
                arrive(self.other(block, which), self.sib_sems, d)

    right = (s, hi * 4 + (x + 1) % 4)
    left = (s, hi * 4 + (x + 3) % 4)

    def shard(block, which):
        h = hi if which == 0 else 1 - hi
        return h * 4 + (x + block) % 4

    def shard_rows(block, which):
        return pl.ds(pl.multiple_of(shard(block, which) * 192, 192), 192)

    def whole_ring(ref, ring_sems):
        return Ring(lambda block, which: ref.at[shard_rows(block, which)], ring_sems, right, left)

    def half_ring(kind, ref, ring_sems, sib_sems):
        def of(c):
            def piece(block, which):
                first = shard(block, which) * 192 + c * 96
                return ref.at[pl.ds(pl.multiple_of(first, 96), 96)]

            return piece

        return kind(of(core), ring_sems, right, left, of(1 - core), sib_sems)

    def seq_peer(d):
        return (2 * ((j + d) % 8) + core, m)

    my_rows = shard_rows(0, 0)
    own_half = pl.ds(pl.multiple_of(core * 96, 96), 96)
    widen_half = pl.ds(pl.multiple_of(core * 768, 768), 768)
    conv_half = pl.ds(pl.multiple_of(core * 48, 48), 48)
    other_widen_half = pl.ds(pl.multiple_of((1 - core) * 768, 768), 768)
    other_conv_half = pl.ds(pl.multiple_of((1 - core) * 48, 48), 48)

    local = [
        pltpu.make_async_copy(src, dst, in_sem.at[i])
        for i, (src, dst) in enumerate(
            [
                (codes_hbm, codes_i),
                (e_hbm, e_loc),
                (w_hbm, w_loc),
                (exit_hbm, exit_full.at[my_rows]),
                (narrow_hbm, narrow_loc),
                (widen_hbm, widen_all.at[hi]),
                (conv_hbm, conv_all.at[hi]),
            ]
        )
    ]
    for copy in local:
        copy.start()

    x_e = half_ring(Ring, et_full, e_sems, ef_sems)
    x_exit = half_ring(Ring, exit_full, x_sems, xf_sems)
    x_att = whole_ring(att_full, att_sems)
    x_fin = whole_ring(fin_full, fin_sems)

    barrier = pltpu.get_barrier_semaphore()
    greet = [(sib, m), (s8, m4)]
    greet += [(s, (m + d) % 8) for d in range(1, 8)]
    greet += [seq_peer(d) for d in range(1, 8)]
    for dev in greet:
        pl.semaphore_signal(barrier, inc=1, device_id=dev, device_id_type=MESH)

    rows = lax.broadcasted_iota(jnp.int32, (T, T), 0)
    cols = lax.broadcasted_iota(jnp.int32, (T, T), 1)
    order = jnp.where(rows == 4 * (cols % PATCH) + cols // PATCH, 1.0, 0.0).astype(BF)
    local[0].wait()
    codes_all[j] = codes_i[...].astype(BF)
    local[1].wait()
    et_full[my_rows, :] = dot(e_loc[...], order).astype(BF)

    local[2].wait()
    gain = g1_ref[...].astype(F32).reshape(1, D)
    wg_t[0:448, :] = (w_loc[...].astype(F32) * gain).astype(BF)
    wg_t[448:512, :] = jnp.zeros((64, D), BF)

    shard_stream = dot_nt(et_full[my_rows, :], one_hot_codes(codes_all[j])).astype(BF).astype(F32)
    squares = jnp.sum(shard_stream * shard_stream, axis=0, keepdims=True)
    sq_all[0] = squares

    pl.semaphore_wait(barrier, len(greet))

    for d in range(1, 8):
        push(sq_all.at[0], sq_all.at[d], sq_sems, d, (s, (m + d) % 8))
    x_e.start(0)
    push(x_e.piece(0, 0), x_e.piece(0, 0), w_sems, 0, (s8, m4))
    for d in (4, 1, 7, 5, 3, 2, 6):
        push(codes_all.at[j], codes_all.at[j], codes_sems, d, seq_peer(d))
    push(codes_all.at[j], codes_sib, codes_sems, 0, (sib, m))
    push(exit_hbm.at[own_half], x_exit.piece(0, 0), w_sems, 1, (s8, m4))
    push(widen_hbm.at[widen_half], widen_all.at[hi, widen_half], w_sems, 2, (s8, m4))

    local[4].wait()
    narrow_t[hi] = narrow_loc[...].T
    arrive(x_e.piece(0, 1), w_sems, 0)
    x_e.start(1)
    x_e.relay(0)
    x_e.relay(1)
    local[3].wait()
    x_exit.start(0)
    for d in range(1, 8):
        arrive(sq_all.at[d], sq_sems, d)
        squares = squares + sq_all[d]
    u_all[j] = squares / D + EPS
    push(u_all.at[j], u_sib, u_sems, 0, (sib, m))
    for d in range(1, 8):
        push(u_all.at[j], u_all.at[j], u_sems, d, seq_peer(d))
    x_e.near()
    x_e.opposite()
    x_e.others()
    arrive(x_exit.piece(0, 1), w_sems, 1)
    x_exit.start(1)

    m_t[...] = dot(wg_t[...], et_full[...]).astype(BF)

    lanes = lax.broadcasted_iota(jnp.int32, (T, 256), 1)

    def keys_values(block, at):
        hot = one_hot_codes(codes_all[block])
        raw = dot_nt(hot, m_t[128:512, :])
        spread = token_columns(u_all[block], 128)
        key = raw[:, :128]
        mean = jnp.mean(key * key, axis=1, keepdims=True)
        keys[at, :] = (key * lax.rsqrt(mean + EPS * spread)).astype(BF)
        inverse = lax.rsqrt(spread)
        value = raw[:, 128:] * jnp.concatenate([inverse, inverse], axis=1)
        vals[at, :] = jnp.where(lanes < VALUE, value, 1.0).astype(BF)

    factor = sharp_ref[0] * (LOG2E / PROBE)

    def make_queries(slot, codes, u_row):
        raw = dot_nt(one_hot_codes(codes), m_t[0:128, :])
        spread = token_columns(u_row, 128)
        mean = jnp.mean(raw * raw, axis=1, keepdims=True)
        queries[slot] = (raw * (lax.rsqrt(mean + EPS * spread) * factor)).astype(BF)

    keys_values(j, pl.ds(0, T))
    make_queries(core, codes_all[j], u_all[j])
    arrive(codes_sib, codes_sems, 0)
    arrive(u_sib, u_sems, 0)
    make_queries(1 - core, codes_sib[...], u_sib[...])
    for d in (4, 1, 7, 5, 3, 2, 6):
        block = (j + 8 - d) % 8
        arrive(codes_all.at[block], codes_sems, d)
        arrive(u_all.at[block], u_sems, d)
        keys_values(block, pl.ds(d * T, T))

    def attend(slot, half):
        asked = queries[slot, pl.ds(pl.multiple_of(half * TH, TH), TH), :]
        weights = jnp.exp2(dot_nt(asked, keys[...])).astype(BF)
        return dot(weights, vals[...])

    def exchange(slot, which):
        part_send[which] = attend(slot, 1 - core)
        push(part_send.at[which], part_recv.at[which], p_sems, which, (sib, m))

    def attended(slot, which):
        whole = attend(slot, core)
        arrive(part_recv.at[which], p_sems, which)
        whole = whole + part_recv[which]
        return (whole[:, :VALUE] / whole[:, VALUE : VALUE + 1]).astype(BF).T

    x_exit.relay(0)
    exchange(1 - hi, 1)
    att_send[...] = attended(1 - hi, 1)
    push(att_send, att_full.at[my_rows], p_sems, 2, (s, m4))
    narrow_mine = narrow_t.at[hi, widen_half]
    push(narrow_mine, narrow_mine, w_sems, 3, (s8, m4))
    push(conv_hbm.at[:, conv_half], conv_all.at[hi, :, conv_half], w_sems, 4, (s8, m4))
    exchange(hi, 0)
    x_exit.relay(1)
    own_attended = attended(hi, 0)
    arrive(att_full.at[shard_rows(0, 1)], p_sems, 2)
    x_att.start(1)
    att_full[my_rows, :] = own_attended
    x_att.start(0)

    foreign_widen = widen_all.at[1 - hi, widen_half]
    arrive(foreign_widen, w_sems, 2)
    push(foreign_widen, foreign_widen, wf_sems, 0, (sib, m))
    x_att.relay(0)

    def group_stream(codes):
        hot = one_hot_codes(codes)

        def step(i, _):
            at = pl.ds(pl.multiple_of(i * 256, 256), 256)
            stream[:, at] = dot_nt(hot, et_full[at, :]).astype(BF)
            return 0

        lax.fori_loop(0, D // 256, step, 0)

    half_rows = pl.ds(pl.multiple_of(core * TH, TH), TH)

    @pl.when(core == hi)
    def _():
        group_stream(codes_all[j, half_rows])

    @pl.when(core != hi)
    def _():
        group_stream(codes_sib[half_rows, :])

    x_att.relay(1)
    x_exit.near()
    x_exit.opposite()
    x_exit.others()
    x_att.near()
    x_att.opposite()
    for b in range(4):
        att[:, b * 384 : (b + 1) * 384] = att_full[b * 384 : (b + 1) * 384, :].T

    def exit_step(i, total):
        at = pl.ds(pl.multiple_of(i * 256, 256), 256)
        tile = (stream[:, at].astype(F32) + dot(att[...], exit_full[:, at])).astype(BF)
        mixed[:, at] = tile
        wide = tile.astype(F32)
        return total + jnp.sum(wide * wide, axis=1, keepdims=True)

    squares = lax.fori_loop(0, D // 256, exit_step, jnp.zeros((TH, 1), F32))
    second_scale = lax.rsqrt(squares / D + EPS)
    gain = g2_ref[...].astype(F32).reshape(1, D)
    scaled = (mixed[...].astype(F32) * gain).astype(BF)
    local[5].wait()
    arrive(widen_all.at[1 - hi, other_widen_half], wf_sems, 0)
    for h in range(2):
        inner = jnp.maximum(dot(scaled, widen_all[h]) * second_scale, 0.0).astype(BF)
        inner_t[h * HIDDEN : (h + 1) * HIDDEN, :] = inner.T

    foreign_narrow = narrow_t.at[1 - hi, widen_half]
    arrive(foreign_narrow, w_sems, 3)
    push(foreign_narrow, foreign_narrow, wf_sems, 1, (sib, m))
    arrive(narrow_t.at[1 - hi, other_widen_half], wf_sems, 1)

    def partial(block, which):
        at = shard_rows(block, which)
        return dot(narrow_t[0, at, :], inner_t[:HIDDEN, :]) + dot(
            narrow_t[1, at, :], inner_t[HIDDEN:, :]
        )

    def give(index, value, dst, d, dev):
        rs_send[index] = value.astype(BF)
        push(rs_send.at[index], dst, sum_sems, d, dev)

    give(0, partial(2, 0), rs_half.at[0], 0, right)
    give(1, partial(2, 1), rs_half.at[1], 1, left)
    give(2, partial(1, 1), rs_recv.at[0, 1], 2, right)
    give(3, partial(3, 0), rs_recv.at[1, 0], 3, left)
    right_sum = partial(1, 0)
    left_sum = partial(3, 1)
    mixed_t[...] = mixed[...].T
    own = [
        partial(0, which) + mixed_t[shard_rows(0, which), :].astype(F32) for which in range(2)
    ]
    arrive(rs_half.at[0], sum_sems, 0)
    give(4, right_sum + rs_half[0].astype(F32), rs_recv.at[0, 0], 4, right)
    arrive(rs_half.at[1], sum_sems, 1)
    give(5, left_sum + rs_half[1].astype(F32), rs_recv.at[1, 1], 5, left)

    def finish(which, from_left, from_right):
        arrive(rs_recv.at[0, which], sum_sems, from_left)
        arrive(rs_recv.at[1, which], sum_sems, from_right)
        total = own[which] + rs_recv[0, which].astype(F32) + rs_recv[1, which].astype(F32)
        fin_full[shard_rows(0, which), :] = total.astype(BF)
        x_fin.start(which)

    finish(0, 4, 3)
    finish(1, 2, 5)

    next_s = (s + 16 + (1 - core) + core * (2 * hi - 1)) % 16
    prev_s = (s + 16 - core + (1 - core) * (2 * hi - 1)) % 16
    ends = [
        fin_full[pl.ds(pl.multiple_of((h * 4 + x) * 192, 192), 192), :] for h in range(2)
    ]
    halo_send[0] = jnp.concatenate([end[:, TH - 128 :].T[112:128] for end in ends], axis=1)
    halo_send[1] = jnp.concatenate([end[:, :128].T[0:16] for end in ends], axis=1)
    sides = [(next_s, (hi + core) % 2), (prev_s, (hi + 1 - core) % 2)]
    for side, (to_s, to_hi) in enumerate(sides):
        for k in range(4):
            push(
                halo_send.at[side],
                halo_recv.at[side * 4 + x],
                edge_sems,
                side * 4 + k,
                (to_s, to_hi * 4 + (x + k) % 4),
            )

    foreign_conv = conv_all.at[1 - hi, :, conv_half]
    arrive(foreign_conv, w_sems, 4)
    push(foreign_conv, foreign_conv, wf_sems, 2, (sib, m))
    x_fin.relay(0)
    x_fin.relay(1)
    local[6].wait()
    arrive(conv_all.at[1 - hi, :, other_conv_half], wf_sems, 2)
    for h in range(2):
        taps = [conv_all[h, k].astype(F32) for k in range(5)]
        folded = [
            (taps[0] + taps[1], taps[0]),
            (taps[2] + taps[3], taps[1] + taps[2]),
            (taps[4], taps[3] + taps[4]),
        ]
        for index, (even, odd) in enumerate(folded):
            conv_t[index, h * 192 : h * 192 + OUTS, :] = even.astype(BF)
            conv_t[index, h * 192 + OUTS : (h + 1) * 192, :] = odd.astype(BF)

    for side in range(2):
        for k in range(4):
            arrive(halo_recv.at[side * 4 + (x + 4 - k) % 4], edge_sems, side * 4 + k)
        row = jnp.concatenate(
            [
                halo_recv[side * 4 + chip][:, h * 192 : (h + 1) * 192]
                for h in range(2)
                for chip in range(4)
            ],
            axis=1,
        )
        added = dot_nt(row, conv_t[2 * side]).T
        column = added[:, 15:16] if side == 0 else added[:, 0:1]
        edges[side] = jnp.broadcast_to(column, (4 * OUTS, 128))

    x_fin.near()
    x_fin.opposite()

    place = 4 * j + 2 * hi + core
    rows = lax.broadcasted_iota(jnp.int32, (256, 256), 0)
    cols = lax.broadcasted_iota(jnp.int32, (256, 256), 1)
    weave = jnp.where(cols == 2 * (rows % 128) + rows // 128, 1.0, 0.0).astype(BF)

    def taps_of(which):
        h = hi if which == 0 else 1 - hi
        at = pl.ds(pl.multiple_of(h * 192, 192), 192)
        return at, [dot(conv_t[k, at, :], fin_full[...]) for k in range(3)]

    def outputs(at, products):
        before, here, after = products
        left_edge = jnp.where(place > 0, edges[0, at, :][:, 0:1], 0.0)
        right_edge = jnp.where(place < 31, edges[1, at, :][:, 0:1], 0.0)
        before = jnp.concatenate([left_edge, before[:, : TH - 1]], axis=1)
        after = jnp.concatenate([after[:, 1:], right_edge], axis=1)
        result = (before + here + after).astype(BF)
        woven = []
        for b in range(2):
            span = slice(b * 128, (b + 1) * 128)
            both = jnp.concatenate([result[:OUTS, span], result[OUTS:, span]], axis=1)
            woven.append(dot(both, weave).astype(BF))
        return jnp.concatenate(woven, axis=1)

    out_send[1] = outputs(*taps_of(1))
    push(out_send.at[1], out_recv.at[core], out_sems, 4 + core, (2 * j + hi, m4))
    mine = outputs(*taps_of(0))
    out_send[0] = mine
    to_sibling = send(out_send.at[0], out_recv.at[core], out_sems, 2 + core, (sib, m))

    @pl.when(core == hi)
    def _():
        out_ref[:, pl.ds(pl.multiple_of(core * T, T), T)] = mine
        arrive(out_recv.at[1 - core], out_sems, 3 - core)
        out_ref[:, pl.ds(pl.multiple_of((1 - core) * T, T), T)] = out_recv[1 - core]

    @pl.when(core != hi)
    def _():
        to_sibling.start()
        arrive(out_recv.at[0], out_sems, 4)
        arrive(out_recv.at[1], out_sems, 5)
        out_ref[:, :T] = out_recv[0]
        out_ref[:, T:] = out_recv[1]
        to_sibling.wait_send()

    for copy in pending:
        copy.wait_send()


def per_device(codes, e, g1, w, sharp, exit_map, g2, widen, narrow, conv):
    any_space = pl.BlockSpec(memory_space=pl.ANY)
    vmem = pl.BlockSpec(memory_space=pltpu.VMEM)
    smem = pl.BlockSpec(memory_space=pltpu.SMEM)
    dma = pltpu.SemaphoreType.DMA((8,))
    return pl.pallas_call(
        kernel,
        out_shape=jax.ShapeDtypeStruct((OUTS, 2 * T), BF),
        in_specs=[
            any_space,
            any_space,
            vmem,
            any_space,
            smem,
            any_space,
            vmem,
            any_space,
            any_space,
            any_space,
        ],
        out_specs=vmem,
        scratch_shapes=[
            pltpu.VMEM((T, PATCH), jnp.int32),
            pltpu.VMEM((8, T, PATCH), BF),
            pltpu.VMEM((T, PATCH), BF),
            pltpu.VMEM((192, T), BF),
            pltpu.VMEM((D, T), BF),
            pltpu.VMEM((448, D), BF),
            pltpu.VMEM((T, D), BF),
            pltpu.VMEM((T, T), BF),
            pltpu.VMEM((D, D), BF),
            pltpu.VMEM((TH, D), BF),
            pltpu.VMEM((8, 1, T), F32),
            pltpu.VMEM((8, 1, T), F32),
            pltpu.VMEM((1, T), F32),
            pltpu.VMEM((8 * T, PROBE), BF),
            pltpu.VMEM((8 * T, 256), BF),
            pltpu.VMEM((2, T, PROBE), BF),
            pltpu.VMEM((2, TH, 256), F32),
            pltpu.VMEM((2, TH, 256), F32),
            pltpu.VMEM((192, TH), BF),
            pltpu.VMEM((D, TH), BF),
            pltpu.VMEM((TH, D), BF),
            pltpu.VMEM((TH, D), BF),
            pltpu.VMEM((D, TH), BF),
            pltpu.VMEM((2, D, HIDDEN), BF),
            pltpu.VMEM((HIDDEN, D), BF),
            pltpu.VMEM((2, D, HIDDEN), BF),
            pltpu.VMEM((2 * HIDDEN, TH), BF),
            pltpu.VMEM((6, 192, TH), BF),
            pltpu.VMEM((2, 192, TH), BF),
            pltpu.VMEM((2, 2, 192, TH), BF),
            pltpu.VMEM((D, TH), BF),
            pltpu.VMEM((2, 5, OUTS, D), BF),
            pltpu.VMEM((3, 4 * OUTS, D), BF),
            pltpu.VMEM((2, 16, 2 * 192), BF),
            pltpu.VMEM((8, 16, 2 * 192), BF),
            pltpu.VMEM((2, 4 * OUTS, 128), F32),
            pltpu.VMEM((2, OUTS, T), BF),
            pltpu.VMEM((2, OUTS, T), BF),
        ]
        + [dma] * 31,
        compiler_params=pltpu.CompilerParams(
            collective_id=0, has_side_effects=True, vmem_limit_bytes=60 * 1024 * 1024
        ),
        cost_estimate=pl.CostEstimate(
            flops=8_000_000_000, bytes_accessed=8_000_000, transcendentals=4_000_000
        ),
        name="genomic_forward",
    )(
        codes.reshape(T, PATCH),
        e.T,
        g1,
        w.T,
        sharp,
        exit_map,
        g2,
        widen,
        narrow,
        conv.transpose(0, 2, 1),
    )


def solution(mesh):
    in_specs = (
        P("seq"),
        P(None, "mp"),
        P(),
        P(None, "mp"),
        P("mp"),
        P("mp", None),
        P(),
        P(None, "mp"),
        P("mp", None),
        P(None, None, "mp"),
    )
    return jax.shard_map(
        per_device, mesh=mesh, in_specs=in_specs, out_specs=P("mp", "seq"), check_vma=False
    )
```
